128 devices in a mesh: lat: 4 (over y_hi, core), lon: 32 (over y_lo, x, z).
Axes of the slice: x: 4, y: 4 (y_hi: 2, y_lo: 2; y = y_hi * 2 + y_lo), z: 4, core: 2. Of those that a mesh axis runs over, the one named last changes fastest.
Arguments:
- latent_field: bfloat16 [2, 192, 1152, 512], P(None, 'lat', 'lon'), may hold values from -6 to 6
- land_mask: int32 [192, 1152], P('lat', 'lon'), may hold values 0 or 1
- padded: int32 [192, 1152], P('lat', 'lon'), may hold values 0 or 1
- norm1_gain: float32 [512], replicated, may hold values from 0.1 to 1.9
- qkv_weight: bfloat16 [512, 1536], replicated, may hold values from -0.25 to 0.25
- land_bias: float32 [16], replicated, may hold values from -2 to 300
- out_weight: bfloat16 [512, 512], replicated, may hold values from -0.25 to 0.25
- norm2_gain: float32 [512], replicated, may hold values from 0.1 to 1.9
- up_weight: bfloat16 [512, 2048], replicated, may hold values from -0.25 to 0.25
- down_weight: bfloat16 [2048, 512], replicated, may hold values from -0.125 to 0.125
Outputs:
- mixed: bfloat16 [2, 192, 1152, 512], P(None, 'lat', 'lon')
The draws below stay inside these ranges and needn't reach their ends.
Inputs may be any that keep to these rules, and one draw needn't show every extreme that they name: `land_mask`: 1 marks land. `padded`: 1 marks a padding cell.
All inputs are finite; a program needn't handle non-finite values. No bound on the sum of `land_mask` or of `padded` on one device may be relied on, other than what follows from the above.
Results may differ from the reference program's by a relative error of at most 0.007.
Values may be sent and summed in bfloat16 or wider, within the bound.
No kernel may reach another device: no remote copies, remote signals or barrier semaphores. Data moves between devices by JAX's collectives and lax.ppermute only.
A program may use at most 192 MiB of HBM per device.

```python
import math
import jax
import jax.numpy as jnp
from jax import lax

D = 512
HEADS = 16
FF = 2048
LEV = 2
WIN = 12
SHIFT = 6
NLAT = 192
NLON = 1152


def draw_land_bias(key, part):
    key = jax.random.fold_in(key, 17)
    key_strong = jax.random.fold_in(key, 0)
    return jax.random.uniform(key_strong, (HEADS,), jnp.float32, -2.0, 2.0)


def place_ends(result, rng, least, largest):
    spot = [jax.random.randint(jax.random.fold_in(rng, axis), (), 0, length) for axis, length in enumerate(result.shape)]
    longest = result.shape.index(max(result.shape))
    next_to = spot[:longest] + [(spot[longest] + 1) % result.shape[longest]] + spot[longest + 1:]
    return result.at[tuple(spot)].set(least).at[tuple(next_to)].set(largest)


def levels(key, dims, cuts, smallest, largest):
    loudness, own = 1.0, jax.random.fold_in(key, 6)
    for axis_at, blocks in cuts:
        steps = jnp.exp(jax.random.uniform(jax.random.fold_in(own, axis_at), (blocks,), jnp.float32, smallest / len(cuts), largest / len(cuts)))
        loudness = loudness * jnp.repeat(steps, dims[axis_at] // blocks).reshape([-1 if axis == axis_at else 1 for axis in range(len(dims))])
    return loudness


def noise(key, extent, width, limit, cuts=(), kind=jnp.bfloat16):
    array = jax.random.normal(key, extent, jnp.float32) * width
    if len(cuts) > 0:
        array = levels(key, extent, cuts, -0.22, 0.18) * array
    return jnp.clip(array, min=-limit, max=limit).astype(kind)


def setup_inputs(seed: int = 0) -> dict:
    key_of = jax.random.split(jax.random.key(seed), 11)
    return {
        "latent_field": noise(key_of[0], (LEV, NLAT, NLON, D), 1.0, 6.0, ((1, 4), (2, 32))),
        "land_mask": place_ends((jax.random.randint(key_of[1], (NLAT, NLON), 0, 10) < 3).astype(jnp.int32), jax.random.fold_in(key_of[1], 1), 0, 1),
        "padded": place_ends((jax.random.randint(key_of[2], (NLAT, NLON), 0, 8) < 1).astype(jnp.int32), jax.random.fold_in(key_of[2], 1), 0, 1),
        "norm1_gain": jnp.clip(1.0 + 0.18 * jax.random.normal(key_of[3], (D,), jnp.float32), 0.1, 1.9),
        "qkv_weight": noise(key_of[4], (D, 3 * D), D ** -0.5, 0.25),
        "land_bias": draw_land_bias(jax.random.fold_in(key_of[10], 71), 0),
        "out_weight": noise(key_of[6], (D, D), D ** -0.5, 0.25),
        "norm2_gain": jnp.clip(1.0 + 0.18 * jax.random.normal(key_of[7], (D,), jnp.float32), 0.1, 1.9),
        "up_weight": noise(key_of[8], (D, FF), D ** -0.5, 0.25),
        "down_weight": noise(key_of[9], (FF, D), FF ** -0.5, 0.125),
    }


def layer_norm(values_in, gain):
    wide = values_in.astype(jnp.float32)
    center = wide - lax.optimization_barrier(jnp.mean(wide, axis=-1, keepdims=True))
    spread = lax.optimization_barrier(jnp.mean(center * center, axis=-1, keepdims=True))
    return (center * lax.rsqrt(spread + 1e-05) * gain).astype(jnp.bfloat16)

def attend_windows(tokens, land_tok, pad_tok, polar_tok, norm1_gain, qkv_weight, land_bias, out_weight):
    windows_n, count, channels = tokens.shape
    heads = land_bias.shape[0]
    head_size = channels // heads
    normed = layer_norm(tokens, norm1_gain)
    packed = jnp.einsum('wnd,de->wne', normed.astype(jnp.float32), qkv_weight.astype(jnp.float32)).astype(jnp.bfloat16)
    packed = packed.reshape(windows_n, count, 3, heads, head_size)
    queries = packed[:, :, 0].astype(jnp.float32)
    key_rows = packed[:, :, 1].astype(jnp.float32)
    val_rows = packed[:, :, 2].astype(jnp.float32)
    scores = jnp.einsum('wqhe,wkhe->whqk', queries, key_rows) * (1.0 / math.sqrt(head_size))
    land_f = land_tok.astype(jnp.float32)
    scores = scores + land_bias[None, :, None, None] * (land_f[:, :, None] * land_f[:, None, :])[:, None]
    same_group = polar_tok[:, :, None] == polar_tok[:, None, :]
    itself = jnp.eye(count, dtype=jnp.bool_)
    allowed = same_group & ((pad_tok[:, None, :] == 0) | itself[None])
    scores = jnp.where(allowed[:, None], scores, -1e+30)
    row_max = lax.optimization_barrier(jnp.max(scores, axis=-1, keepdims=True))
    raised = jnp.exp(scores - row_max)
    attn_weights = (raised / lax.optimization_barrier(jnp.sum(raised, axis=-1, keepdims=True))).astype(jnp.bfloat16)
    heads_out = jnp.einsum('whqk,wkhe->wqhe', attn_weights.astype(jnp.float32), val_rows).astype(jnp.bfloat16)
    heads_out = heads_out.reshape(windows_n, count, channels)
    return jnp.einsum('wnd,de->wne', heads_out.astype(jnp.float32), out_weight.astype(jnp.float32)).astype(jnp.bfloat16)

def reference(latent_field, land_mask, padded, norm1_gain, qkv_weight, land_bias, out_weight, norm2_gain, up_weight, down_weight):
    rolled = jnp.roll(latent_field, (-SHIFT, -SHIFT), (1, 2))
    land_rolled = jnp.roll(land_mask, (-SHIFT, -SHIFT), (0, 1))
    pad_rolled = jnp.roll(padded, (-SHIFT, -SHIFT), (0, 1))
    polar = jnp.roll((jnp.arange(NLAT) < SHIFT).astype(jnp.int32), -SHIFT)
    band_n = NLAT // WIN
    col_n = NLON // WIN
    count = LEV * WIN * WIN
    tiles = rolled.reshape(LEV, band_n, WIN, col_n, WIN, D).transpose(1, 3, 0, 2, 4, 5).reshape(band_n * col_n, 1, count, D)

    def spread_cells(cells):
        arranged = cells.reshape(band_n, WIN, col_n, WIN).transpose(0, 2, 1, 3)[:, :, None]
        return jnp.broadcast_to(arranged, (band_n, col_n, LEV, WIN, WIN)).reshape(band_n * col_n, 1, count)
    land_tok = spread_cells(land_rolled)
    pad_tok = spread_cells(pad_rolled)
    polar_tok = spread_cells(jnp.broadcast_to(polar[:, None], (NLAT, NLON)))

    def one_window(parts):
        return attend_windows(parts[0], parts[1], parts[2], parts[3], norm1_gain, qkv_weight, land_bias, out_weight)
    outcome = lax.map(one_window, (tiles, land_tok, pad_tok, polar_tok))
    attended = outcome.reshape(band_n, col_n, LEV, WIN, WIN, D).transpose(2, 0, 3, 1, 4, 5).reshape(LEV, NLAT, NLON, D)
    attended = jnp.roll(attended, (SHIFT, SHIFT), (1, 2))

    def one_row(parts):
        residual = parts[0].astype(jnp.float32) + parts[1].astype(jnp.float32)
        normed = layer_norm(residual, norm2_gain).reshape(-1, D)
        hidden = jax.nn.gelu(jnp.dot(normed, up_weight, preferred_element_type=jnp.float32), approximate=False).astype(jnp.bfloat16)
        output = residual + jnp.dot(hidden, down_weight, preferred_element_type=jnp.float32).reshape(residual.shape)
        return output.astype(jnp.bfloat16)
    mixed = lax.map(one_row, (latent_field.transpose(1, 0, 2, 3), attended.transpose(1, 0, 2, 3)))
    return mixed.transpose(1, 0, 2, 3)
```

```python
import math, functools
import jax, jax.numpy as jnp
from jax import lax
from jax.experimental import pallas as pl
from jax.experimental.pallas import tpu as pltpu

F32, BF16 = jnp.float32, jnp.bfloat16
LOG2E = math.log2(math.e)
D, HEADS, FF = 512, 16, 2048
SCALE = LOG2E / math.sqrt(32.0)
W = 288
NEG = -1e30

def dot(a, b):
    return lax.dot_general(a, b, (((1,), (0,)), ((), ())), preferred_element_type=F32)

def dot_t(a, b):
    return lax.dot_general(a, b, (((1,), (1,)), ((), ())), preferred_element_type=F32)

def norm(x, g):
    c = x - jnp.mean(x, axis=-1, keepdims=True)
    s = jnp.mean(c * c, axis=-1, keepdims=True)
    return c * lax.rsqrt(s + 1e-5) * g

def lanes(shape):
    return lax.broadcasted_iota(jnp.int32, shape, len(shape) - 1)

def rows(shape):
    return lax.broadcasted_iota(jnp.int32, shape, len(shape) - 2)

def gelu(x):
    return 0.5 * x * (1.0 + lax.erf(x * (1 / math.sqrt(2.0))))

def split3(v):
    hi = v.astype(BF16).astype(F32)
    mid = (v - hi).astype(BF16).astype(F32)
    return hi, mid, v - hi - mid

def bias_lanes(b, n):
    hi, mid, lo = split3(jnp.full((1, 128), b * LOG2E, F32))
    at = lanes((1, 128))
    return jnp.where(at == 0, hi, jnp.where(at == 1, mid, jnp.where(at == 2, lo, 0.0)))

def attend(nq, q_of, k_of, v_of, land_q, land_k, mask, mask_tail, bias_ref, qs, ke, kt, s_ref, t_ref, p_ref, ve, heads_out, ho_row):
    seg = lanes((1, 128)) // 32
    three = (lanes((1, 128)) < 3).astype(F32)
    for g in range(4):
        b = g % 2
        q = q_of(g)
        k = k_of(g)
        v = v_of(g)
        kland = (land_k * three).astype(BF16)
        ke[b, :, 0:128] = k
        ke[b, :, 128:256] = kland
        qland = land_q
        for h in range(4):
            hm = (seg == h)
            qs[b, h * nq:(h + 1) * nq, 0:128] = jnp.where(hm, q, 0.0).astype(BF16)
            qs[b, h * nq:(h + 1) * nq, 128:256] = (qland * bias_lanes(bias_ref[4 * g + h], 128)).astype(BF16)
            hmb = hm.astype(BF16)
            ve[b, h * 256:(h + 1) * 256, 0:128] = v[0:256] * hmb
            ve[b, h * 256:(h + 1) * 256, 128:256] = jnp.broadcast_to(hmb, (256, 128))
            ve[b, 1024 + 32 * h:1056 + 32 * h, 0:128] = v[256:288] * hmb
            ve[b, 1024 + 32 * h:1056 + 32 * h, 128:256] = jnp.broadcast_to(hmb, (32, 128))
            kt[b, 32 * h:32 * h + 32, 0:128] = k[256:288] * hmb
            kt[b, 32 * h:32 * h + 32, 128:256] = (land_k[256:288] * bias_lanes(bias_ref[4 * g + h], 128)).astype(BF16)
        qs[b, 4 * nq:5 * nq, 0:128] = q.astype(BF16)
        qs[b, 4 * nq:5 * nq, 128:256] = (land_q * three).astype(BF16)
        s_ref[b, 0:4 * nq] = dot_t(qs[b, 0:4 * nq], ke[b, 0:256])
        t_ref[b, 0:nq] = dot_t(qs[b, 4 * nq:5 * nq], kt[b])
        R = 16
        for r in range(0, nq, R):
            rr = min(R, nq - r)
            t = t_ref[b, r:r + rr] + mask_tail[r:r + rr]
            mk = mask[r:r + rr]
            ms = []
            for h in range(4):
                s = s_ref[b, h * nq + r:h * nq + r + rr] + mk
                m = jnp.maximum(jnp.maximum(s[:, :128], s[:, 128:]), jnp.where(seg == h, t, -3e38))
                m = jnp.max(m, axis=-1, keepdims=True)
                p_ref[b, r:r + rr, h * 256:(h + 1) * 256] = jnp.exp2(s - m).astype(BF16)
                ms.append(m)
            mt = jnp.where(seg == 0, ms[0], jnp.where(seg == 1, ms[1], jnp.where(seg == 2, ms[2], ms[3])))
            p_ref[b, r:r + rr, 1024:1152] = jnp.exp2(t - mt).astype(BF16)
        o = dot(p_ref[b, 0:nq], ve[b])
        heads_out[pl.ds(ho_row, nq), g * 128:(g + 1) * 128] = (o[:, :128] / o[:, 128:]).astype(BF16)

def k1_body(x, land, pad, g1, wqkv, bias, wout, g2, wup, wdown, out, edge, xg, qkv, ho, qs, ke, kt, s_ref, t_ref, p_ref, ve, mk, mkt, att, nat, skip=()):
    gain1 = g1[...]
    if "ln" not in skip:
      @pl.loop(0, 24)
      def _(n):
        l, m = n // 12, n % 12
        jc, p = m // 6, m % 6
        for two in range(2):
            v = norm(x[l, 6 + jc * 12 + 2 * p + two].astype(F32), gain1)
            for i in range(3):
                w = jc * 3 + i
                row = pl.multiple_of(l * 144 + 24 * p, 8)
                xg.at[w, pl.ds(row, 24), :][12 * two:12 * two + 12, :] = v[6 + 12 * i:18 + 12 * i]
    if "qkv" not in skip:
      @pl.loop(0, 6)
      def _(w):
        xn = xg[w].astype(BF16)
        for c in range(6):
            r = dot(xn, wqkv[:, c * 256:(c + 1) * 256])
            if c < 2:
                r = r * SCALE
            qkv[w, :, c * 256:(c + 1) * 256] = r.astype(BF16)
    if "att" not in skip:
      @pl.loop(0, 6)
      def _(w):
        jc, i = w // 3, w % 3
        at_c = rows((36, W))
        lane = lanes((1, W)) % 144
        here = at_c == (6 + jc * 12 + lane // 12)
        pick = (rows((48, W)) == (6 + i * 12 + lane % 12)).astype(BF16)
        landrow = jnp.sum(jnp.where(here, dot(land[...].astype(F32).astype(BF16), pick), 0.0), axis=0, keepdims=True)
        padrow = jnp.sum(jnp.where(here, dot(pad[...].astype(F32).astype(BF16), pick), 0.0), axis=0, keepdims=True)
        eye = rows((W, W)) == lanes((W, W))
        land_k = jnp.broadcast_to(jnp.sum(jnp.where(eye, landrow, 0.0), axis=1, keepdims=True), (W, 128))
        mm = jnp.where(eye, 0.0, padrow * NEG)
        mk[...] = mm[:, 0:256]
        mkt[...] = jnp.concatenate([mm[:, 256:288]] * 4, axis=1)
        attend(W, lambda g: qkv[w, :, g * 128:(g + 1) * 128].astype(F32),
               lambda g: qkv[w, :, 512 + g * 128:512 + (g + 1) * 128],
               lambda g: qkv[w, :, 1024 + g * 128:1024 + (g + 1) * 128],
               land_k, land_k, mk, mkt, bias, qs, ke, kt, s_ref, t_ref, p_ref, ve, ho, pl.multiple_of(w * W, 32))
    if "op" not in skip:
      @pl.loop(0, 6)
      def _(w):
        h = ho[pl.ds(pl.multiple_of(w * W, 32), W), :]
        for c in range(2):
            att[w, :, c * 256:(c + 1) * 256] = dot(h, wout[:, c * 256:(c + 1) * 256])
    if "sc" not in skip:
      @pl.loop(0, 24)
      def _(n):
        l, m = n // 12, n % 12
        jc, p = m // 6, m % 6
        for two in range(2):
            c = jc * 12 + 2 * p + two
            for i in range(3):
                w = jc * 3 + i
                row = pl.multiple_of(l * 144 + 24 * p, 8)
                nat[l * 24 + c, 6 + 12 * i:18 + 12 * i, :] = att.at[w, pl.ds(row, 24), :][12 * two:12 * two + 12, :]
            nat[l * 24 + c] = nat[l * 24 + c] + x[l, 6 + c].astype(F32)
            edge[l * 24 + c, 0] = nat[l * 24 + c, 0:8]
            edge[l * 24 + c, 1] = nat[l * 24 + c, 40:48]
    gain2 = g2[...]
    if "ffn" not in skip:
      CH = 12
      @pl.loop(0, 48 // CH)
      def _(n):
        res = nat[pl.ds(n * CH, CH), 8:40, :].reshape(CH * 32, 512)
        xn = norm(res, gain2).astype(BF16)
        acc = res
        for c in range(4):
            hid = gelu(dot(xn, wup[:, c * 512:(c + 1) * 512])).astype(BF16)
            acc = acc + dot(hid, wdown[c * 512:(c + 1) * 512, :])
        out[pl.ds(n * CH, CH)] = acc.astype(BF16).reshape(CH, 32, 512)

def k1(xt, landt, padt, g1, wqkv, bias, wout, g2, wup, wdown, skip=()):
    vm = pl.BlockSpec(memory_space=pltpu.VMEM)
    sm = pl.BlockSpec(memory_space=pltpu.SMEM)
    return pl.pallas_call(
        functools.partial(k1_body, skip=skip),
        out_shape=[jax.ShapeDtypeStruct((48, 32, 512), BF16), jax.ShapeDtypeStruct((48, 2, 8, 512), F32)],
        in_specs=[vm, vm, vm, vm, vm, sm, vm, vm, vm, vm],
        out_specs=[vm, vm],
        scratch_shapes=[
            pltpu.VMEM((6, W, 512), F32),
            pltpu.VMEM((6, W, 1536), BF16),
            pltpu.VMEM((6 * W, 512), BF16),
            pltpu.VMEM((2, 5 * W, 256), BF16),
            pltpu.VMEM((2, W, 256), BF16),
            pltpu.VMEM((2, 128, 256), BF16),
            pltpu.VMEM((2, 4 * W, 256), F32),
            pltpu.VMEM((2, W, 128), F32),
            pltpu.VMEM((2, W, 1152), BF16),
            pltpu.VMEM((2, 1152, 256), BF16),
            pltpu.VMEM((W, 256), F32),
            pltpu.VMEM((W, 128), F32),
            pltpu.VMEM((6, W, 512), F32),
            pltpu.VMEM((48, 48, 512), F32),
        ],
        compiler_params=pltpu.CompilerParams(vmem_limit_bytes=60 * 1024 * 1024),
    )(xt, landt, padt, g1.reshape(1, 512), wqkv, bias, wout, g2.reshape(1, 512), wup, wdown)

import numpy as np
from jax.sharding import PartitionSpec as P


def edge_windows():
    tens = [(i, j) for i in (1, 2, 3) for j in (0, 3)] + [(i, j) for i in (0, 4) for j in (1, 2)]
    return tens + [(i, j) for i in (0, 4) for j in (0, 3)]


def pieces(i, j):
    halves = {0: ((6, 6), (0, 6)), 4: ((48, 6), (54, 6))}.get(i, ((12 * i, 12),))
    cols = {0: (range(6, 12), range(0, 6)), 3: (range(36, 42), range(42, 48))}.get(j, (range(12 * j, 12 * j + 12),))
    return [(l, e, f, n) for es in cols for f, n in halves for l in range(2) for e in es]


def cell_maps():
    e_of, f_of = [], []
    for i, j in edge_windows():
        e_of.append([e for l, e, f, n in pieces(i, j) for _ in range(n)])
        f_of.append([f + a for l, e, f, n in pieces(i, j) for a in range(n)])
    return np.array(e_of, np.int32)[:, None], np.array(f_of, np.int32)[:, None]


def k2_body(flags, e_map, f_map, land, pad, x, left, right, up, down, ul, ur, dl, dr, inner, edge,
            g1, wqkv, bias, wout, g2, wup, wdown, out,
            xg, qkv, ho, qs, ke, kt, s_ref, t_ref, p_ref, ve, mk, mkt, att, nat_s, nat_i):
    wins = edge_windows()

    def column(l, e, f):
        if f < 6:
            return (ul, l, e) if e < 6 else (up, l, e - 6) if e < 42 else (ur, l, e - 42)
        if f >= 54:
            return (dl, l, e) if e < 6 else (down, l, e - 6) if e < 42 else (dr, l, e - 42)
        return (left, l, e) if e < 6 else (x, l, e - 6) if e < 42 else (right, l, e - 42)

    for w, (i, j) in enumerate(wins):
        row = 0
        for l, e, f, n in pieces(i, j):
            ref, a, b = column(l, e, f)
            start = 0 if f < 6 or f >= 54 else f - 6
            xg[w, row:row + n, :] = ref[a, b].astype(F32)[start:start + n]
            row += n
    gain1 = g1[...]

    @pl.loop(0, 14)
    def _(w):
        xn = norm(xg[w], gain1).astype(BF16)
        for c in range(2):
            qkv[w, 0:144, c * 256:(c + 1) * 256] = (dot(xn[0:144], wqkv[:, c * 256:(c + 1) * 256]) * SCALE).astype(BF16)
        for c in range(2, 6):
            qkv[w, :, c * 256:(c + 1) * 256] = dot(xn, wqkv[:, c * 256:(c + 1) * 256]).astype(BF16)

    def window(w, nq):
        here = rows((48, W)) == e_map[w]
        pick = (rows((64, W)) == f_map[w]).astype(BF16)
        landrow = jnp.sum(jnp.where(here, dot(land[...].astype(F32).astype(BF16), pick), 0.0), axis=0, keepdims=True)
        padrow = jnp.sum(jnp.where(here, dot(pad[...].astype(F32).astype(BF16), pick), 0.0), axis=0, keepdims=True)
        f_row = f_map[w]
        over = ((f_row < 6) & (flags[0] > 0)) | ((f_row >= 54) & (flags[1] > 0))
        blocked = jnp.where(over | (padrow > 0.5), NEG, 0.0)
        eye = rows((W, W)) == lanes((W, W))
        land_k = jnp.broadcast_to(jnp.sum(jnp.where(eye, landrow, 0.0), axis=1, keepdims=True), (W, 128))
        mm = jnp.where(rows((nq, W)) == lanes((nq, W)), 0.0, blocked)
        mk[0:nq] = mm[:, 0:256]
        mkt[0:nq] = jnp.concatenate([mm[:, 256:288]] * 4, axis=1)
        attend(nq, lambda g: qkv[w, 0:nq, g * 128:(g + 1) * 128].astype(F32),
               lambda g: qkv[w, :, 512 + g * 128:512 + (g + 1) * 128],
               lambda g: qkv[w, :, 1024 + g * 128:1024 + (g + 1) * 128],
               land_k[0:nq], land_k, mk, mkt, bias, qs, ke, kt, s_ref, t_ref, p_ref, ve, ho, pl.multiple_of(w * 144, 16))

    @pl.loop(0, 10)
    def _(w):
        window(w, 144)

    @pl.loop(10, 14)
    def _(w):
        window(w, 72)

    @pl.loop(0, 7)
    def _(n):
        h = ho[pl.ds(pl.multiple_of(n * 288, 32), 288), :]
        for c in range(2):
            a = dot(h, wout[:, c * 256:(c + 1) * 256])
            att[2 * n, :, c * 256:(c + 1) * 256] = a[0:144]
            att[2 * n + 1, :, c * 256:(c + 1) * 256] = a[144:288]

    side = {c: s for s, c in enumerate(list(range(6)) + list(range(30, 36)))}
    for w, (i, j) in enumerate(wins):
        row = 0
        for l, e, f, n in pieces(i, j):
            if row == (144 if w < 10 else 72):
                break
            c, r = e - 6, f - 6
            seg = att[w, row:row + n, :]
            if c in side:
                nat_s[l * 12 + side[c], r:r + n, :] = seg
            elif r == 0:
                nat_i[l * 24 + c - 6, 0, 0:6, :] = seg
            else:
                nat_i[l * 24 + c - 6, 1, 2:8, :] = seg
            row += n
    gain2 = g2[...]

    def ffn(res):
        xn = norm(res, gain2).astype(BF16)
        acc = res
        for c in range(4):
            hid = gelu(dot(xn, wup[:, c * 512:(c + 1) * 512])).astype(BF16)
            acc = acc + dot(hid, wdown[c * 512:(c + 1) * 512, :])
        return acc.astype(BF16)

    @pl.loop(0, 4)
    def _(n):
        l = n // 2
        c0 = 30 * (n % 2)
        res = nat_s[pl.ds(6 * n, 6)] + x[l, pl.ds(c0, 6)].astype(F32)
        out[l, pl.ds(c0, 6)] = ffn(res.reshape(288, 512)).reshape(6, 48, 512)

    @pl.loop(0, 4)
    def _(n):
        l = n // 2
        c0 = 12 * (n % 2)
        xs = x[l, pl.ds(6 + c0, 12)].astype(F32)
        at = nat_i[pl.ds(12 * n, 12)]
        ed = edge[pl.ds(12 * n, 12)]
        low = jnp.where(rows((1, 8, 512)) < 6, at[:, 0] + xs[:, 0:8], ed[:, 0])
        high = jnp.where(rows((1, 8, 512)) >= 2, at[:, 1] + xs[:, 40:48], ed[:, 1])
        res = jnp.concatenate([low.reshape(96, 512), high.reshape(96, 512)], axis=0)
        y = ffn(res).astype(F32)
        full = jnp.concatenate([y[0:96].reshape(12, 8, 512), inner[pl.ds(12 * n, 12)].astype(F32), y[96:192].reshape(12, 8, 512)], axis=1)
        out[l, pl.ds(6 + c0, 12)] = full.astype(BF16)


def k2(flags, land, pad, xt, halos, inner, edge, g1, wqkv, bias, wout, g2, wup, wdown):
    vm = pl.BlockSpec(memory_space=pltpu.VMEM)
    sm = pl.BlockSpec(memory_space=pltpu.SMEM)
    e_map, f_map = cell_maps()
    return pl.pallas_call(
        k2_body,
        out_shape=jax.ShapeDtypeStruct((2, 36, 48, 512), BF16),
        in_specs=[sm] + [vm] * 17 + [sm] + [vm] * 4,
        out_specs=vm,
        scratch_shapes=[
            pltpu.VMEM((14, W, 512), F32),
            pltpu.VMEM((14, W, 1536), BF16),
            pltpu.VMEM((14 * 144, 512), BF16),
            pltpu.VMEM((2, 5 * 144, 256), BF16),
            pltpu.VMEM((2, W, 256), BF16),
            pltpu.VMEM((2, 128, 256), BF16),
            pltpu.VMEM((2, 4 * 144, 256), F32),
            pltpu.VMEM((2, 144, 128), F32),
            pltpu.VMEM((2, 144, 1152), BF16),
            pltpu.VMEM((2, 1152, 256), BF16),
            pltpu.VMEM((144, 256), F32),
            pltpu.VMEM((144, 128), F32),
            pltpu.VMEM((14, 144, 512), F32),
            pltpu.VMEM((24, 48, 512), F32),
            pltpu.VMEM((48, 2, 8, 512), F32),
        ],
        compiler_params=pltpu.CompilerParams(vmem_limit_bytes=62 * 1024 * 1024),
    )(flags, jnp.asarray(e_map), jnp.asarray(f_map), land, pad, xt, *halos, inner, edge,
      g1.reshape(1, 512), wqkv, bias, wout, g2.reshape(1, 512), wup, wdown)


def from_behind(value, axis, by):
    devices = lax.axis_size(axis)
    return lax.ppermute(value, axis, [(i, (i + by) % devices) for i in range(devices)])


def from_corner(value, by_lat, by_lon):
    n, m = lax.axis_size("lat"), lax.axis_size("lon")
    pairs = [(a * m + b, (a + by_lat) % n * m + (b + by_lon) % m) for a in range(n) for b in range(m)]
    return lax.ppermute(value, ("lat", "lon"), pairs)


def on_device(latent_field, land_mask, padded, norm1_gain, qkv_weight, land_bias, out_weight, norm2_gain, up_weight, down_weight):
    xt = latent_field.transpose(0, 2, 1, 3)
    masks = jnp.stack([land_mask.T, padded.T])
    left = from_behind(xt[:, 30:36], "lon", 1)
    right = from_behind(xt[:, 0:6], "lon", -1)
    up = from_behind(xt[:, :, 42:48], "lat", 1)
    down = from_behind(xt[:, :, 0:6], "lat", -1)
    ul = from_corner(xt[:, 30:36, 42:48], 1, 1)
    ur = from_corner(xt[:, 0:6, 42:48], 1, -1)
    dl = from_corner(xt[:, 30:36, 0:6], -1, 1)
    dr = from_corner(xt[:, 0:6, 0:6], -1, -1)
    tall = jnp.concatenate([from_behind(masks[:, :, 42:48], "lat", 1), masks, from_behind(masks[:, :, 0:6], "lat", -1)], 2)
    wide = jnp.concatenate([from_behind(tall[:, 30:36], "lon", 1), tall, from_behind(tall[:, 0:6], "lon", -1)], 1)
    wide = jnp.pad(wide, ((0, 0), (0, 0), (0, 4)))
    lat = lax.axis_index("lat")
    flags = jnp.stack([(lat == 0).astype(jnp.int32), (lat == lax.axis_size("lat") - 1).astype(jnp.int32)])
    inner, edge = k1(xt, masks[0], masks[1], norm1_gain, qkv_weight, land_bias, out_weight, norm2_gain, up_weight, down_weight)
    y = k2(flags, wide[0], wide[1], xt, (left, right, up, down, ul, ur, dl, dr), inner, edge,
           norm1_gain, qkv_weight, land_bias, out_weight, norm2_gain, up_weight, down_weight)
    return y.transpose(0, 2, 1, 3)


def solution(mesh):
    spec = P(None, "lat", "lon", None)
    placed = (spec, P("lat", "lon"), P("lat", "lon")) + (P(),) * 7
    return jax.shard_map(on_device, mesh=mesh, in_specs=placed, out_specs=spec, check_vma=False)
```

```python
import functools
import math

import jax
import jax.numpy as jnp
import numpy as np
from jax import lax
from jax.experimental import pallas as pl
from jax.experimental.pallas import tpu as pltpu
from jax.sharding import PartitionSpec as P

F32, BF16 = jnp.float32, jnp.bfloat16
LOG2E = math.log2(math.e)
SCALE = LOG2E / math.sqrt(32.0)
W = 288
HALO = 576
PAY = HALO + 16
NEG = -1e30
MB = 1024 * 1024


def dot(a, b):
    return lax.dot_general(a, b, (((1,), (0,)), ((), ())), preferred_element_type=F32)


def dot_t(a, b):
    return lax.dot_general(a, b, (((1,), (1,)), ((), ())), preferred_element_type=F32)


def norm(x, g):
    c = x - jnp.mean(x, axis=-1, keepdims=True)
    s = jnp.mean(c * c, axis=-1, keepdims=True)
    return (c * lax.rsqrt(s + 1e-5) * g).astype(BF16)


def lanes(shape):
    return lax.broadcasted_iota(jnp.int32, shape, len(shape) - 1)


def rows(shape):
    return lax.broadcasted_iota(jnp.int32, shape, len(shape) - 2)


def gelu(x):
    return 0.5 * x * (1.0 + lax.erf(x * (1 / math.sqrt(2.0))))


def halves(cells):
    return cells[...].astype(F32).astype(BF16)


def attend_scratch(nq):
    return [
        pltpu.VMEM((8, 128), F32),
        pltpu.VMEM((2, 4, 4 * nq, 128), BF16),
        pltpu.VMEM((2, nq, 512), BF16),
        pltpu.VMEM((2, W, 512), BF16),
        pltpu.VMEM((2, 4, 1152, 128), BF16),
        pltpu.VMEM((2, 4 * nq, 128), BF16),
        pltpu.VMEM((2, W, 128), F32),
        pltpu.VMEM((2, nq, 256), F32),
        pltpu.VMEM((2, nq, 128), F32),
        pltpu.VMEM((1152, 128), BF16),
        *[pltpu.VMEM((4 * nq, 256), F32)] * 2,
        *[pltpu.VMEM((nq, 128), F32)] * 2,
        *[pltpu.VMEM((nq, 1152), BF16)] * 2,
    ]


def attend_setup(bias_ref, brow, ones):
    at = lanes((1, 128))
    for g in range(4):
        line = jnp.zeros((1, 128), F32)
        for h in range(4):
            full = jnp.full((1, 128), bias_ref[4 * g + h] * LOG2E, F32)
            hi = full.astype(BF16).astype(F32)
            mid = (full - hi).astype(BF16).astype(F32)
            for n, part in enumerate((hi, mid, full - hi - mid)):
                line = jnp.where(at == 3 * h + n, part, line)
        brow[g:g + 1] = line
    for h in range(4):
        hm = (at // 32 == h).astype(BF16)
        ones[256 * h:256 * h + 256] = jnp.broadcast_to(hm, (256, 128))
        ones[1024 + 32 * h:1056 + 32 * h] = jnp.broadcast_to(hm, (32, 128))


def pair(ws, own, tokens, land_row, blocked_row, gain, wqkv, out_row, ho, scratch):
    brow, qst, qpl, kpl, vst, lqx, lk, mk, mkt, ones, s0, s1, t0, t1, p0, p1 = scratch
    nq = qpl.shape[1]
    spot = lanes((1, 128))
    hms = [(spot // 32 == h).astype(BF16) for h in range(4)]
    threes = [(spot // 3 == h).astype(BF16) for h in range(4)]
    xn = jnp.concatenate([norm(tokens[w], gain) for w in ws], axis=0)
    xq = xn if nq == W else jnp.concatenate([xn[0:nq], xn[W:W + nq]], axis=0)
    for c in range(6):
        cols = slice(c * 256, (c + 1) * 256)
        if c < 2:
            r = (dot(xq, wqkv[:, cols]) * SCALE).astype(BF16)
            for a in range(2):
                ra = r[a * nq:(a + 1) * nq]
                qpl[a, :, cols] = ra
                for gl in range(2):
                    for h in range(4):
                        qst[a, 2 * c + gl, h * nq:(h + 1) * nq] = ra[:, gl * 128:(gl + 1) * 128] * hms[h]
        else:
            r = dot(xn, wqkv[:, cols]).astype(BF16)
            for a in range(2):
                ra = r[a * W:(a + 1) * W]
                if c < 4:
                    kpl[a, :, (c - 2) * 256:(c - 1) * 256] = ra
                    continue
                for gl in range(2):
                    g = 2 * (c - 4) + gl
                    for h in range(4):
                        vm = ra[:, gl * 128:(gl + 1) * 128] * hms[h]
                        vst[a, g, 256 * h:256 * h + 256] = vm[0:256]
                        vst[a, g, 1024 + 32 * h:1056 + 32 * h] = vm[256:288]
    eye = rows((W, W)) == lanes((W, W))
    for a, w in enumerate(ws):
        land = jnp.broadcast_to(jnp.sum(jnp.where(eye, land_row(w), 0.0), axis=1, keepdims=True), (W, 128))
        lk[a] = land
        lq = land[0:nq].astype(BF16)
        for h in range(4):
            lqx[a, h * nq:(h + 1) * nq] = lq * threes[h]
        mm = jnp.where(eye[0:nq], 0.0, blocked_row(w))
        mk[a] = mm[:, 0:256]
        mkt[a] = jnp.concatenate([mm[:, 256:288]] * 4, axis=1)

    ss, ts, ps = (s0, s1), (t0, t1), (p0, p1)

    def q_step(n):
        a, g, b = n // 4, n % 4, n % 2
        k = kpl[a, :, g * 128:(g + 1) * 128]
        kx = (lk[a] * brow[g:g + 1]).astype(BF16)
        ss[b][...] = dot_t(jnp.concatenate([qst[a, g], lqx[a]], axis=1), jnp.concatenate([k[0:256], kx[0:256]], axis=1))
        kt = jnp.concatenate([
            jnp.concatenate([k[256:288] * hms[h] for h in range(4)], axis=0),
            jnp.concatenate([kx[256:288] * threes[h] for h in range(4)], axis=0)], axis=1)
        lq = lk[a, 0:nq].astype(BF16)
        ts[b][...] = dot_t(jnp.concatenate([qpl[a, :, g * 128:(g + 1) * 128], lq], axis=1), kt)

    def s_step(n):
        a, b = n // 4, n % 2
        for r in range(0, own, 16):
            at = slice(r, min(r + 16, own))
            size = at.stop - r
            t = ts[b][at] + mkt[a, at]
            mask = mk[a, at]
            tops = []
            for h in range(4):
                s = ss[b][h * nq + r:h * nq + r + size] + mask
                m = jnp.maximum(jnp.maximum(s[:, :128], s[:, 128:]), jnp.where(spot // 32 == h, t, -3e38))
                m = jnp.max(m, axis=-1, keepdims=True)
                ps[b][at, h * 256:(h + 1) * 256] = jnp.exp2(s - m).astype(BF16)
                tops.append(m)
            top = jnp.where(spot < 32, tops[0], jnp.where(spot < 64, tops[1], jnp.where(spot < 96, tops[2], tops[3])))
            ps[b][at, 1024:1152] = jnp.exp2(t - top).astype(BF16)

    def v_step(n):
        a, g, b = n // 4, n % 4, n % 2
        o = dot(ps[b][0:own], jnp.concatenate([vst[a, g], ones[...]], axis=1))
        ho[pl.ds(out_row(ws[a]), own), g * 128:(g + 1) * 128] = (o[:, :128] / o[:, 128:]).astype(BF16)

    for n in range(10):
        if n < 8:
            q_step(n)
        if 1 <= n < 9:
            s_step(n - 1)
        if n >= 2:
            v_step(n - 2)


def feed_forward(res, gain, wup, wdown):
    xn = norm(res, gain)
    acc = res
    for c in range(4):
        hidden = gelu(dot(xn, wup[:, c * 512:(c + 1) * 512])).astype(BF16)
        acc = acc + dot(hidden, wdown[c * 512:(c + 1) * 512, :])
    return acc.astype(BF16)


def fetch(pairs, sems):
    copies = [pltpu.make_async_copy(src, dst, sems.at[n]) for n, (src, dst) in enumerate(pairs)]
    for c in copies:
        c.start()
    return copies


def pack_lon_body(first, last, land, pad, to_right, to_left):
    for strip, c0, to in ((last, 30, to_right), (first, 0, to_left)):
        to[0:HALO] = strip[...].reshape(HALO, 512)
        zero = jnp.zeros((10, 128), F32)
        a = jnp.concatenate([land[c0:c0 + 6].astype(F32), jnp.zeros((6, 80), F32)], axis=1)
        b = jnp.concatenate([pad[c0:c0 + 6].astype(F32), jnp.zeros((6, 80), F32)], axis=1)
        a = jnp.concatenate([a, zero], axis=0)
        b = jnp.concatenate([b, zero], axis=0)
        to[HALO:PAY] = jnp.concatenate([a, b, jnp.zeros((16, 256), F32)], axis=1).astype(BF16)


def wide_masks(land, pad, left, right, wide):
    l, r = left[HALO:PAY].astype(F32), right[HALO:PAY].astype(F32)
    for n, own in enumerate((land, pad)):
        wide[n, 0:6, 0:48] = l[0:6, 128 * n:128 * n + 48]
        wide[n, 6:42, 0:48] = own[...].astype(F32)
        wide[n, 42:48, 0:48] = r[0:6, 128 * n:128 * n + 48]


def pack_lat_body(x_low, x_high, left, right, land, pad, to_down, to_up, buf, wide):
    wide_masks(land, pad, left, right, wide)
    for to, xs, r0 in ((to_down, x_high, 42), (to_up, x_low, 0)):
        x0 = 10 if r0 else 0
        for l in range(2):
            for e in range(48):
                row = 6 * (48 * l + e)
                if e < 6 or e >= 42:
                    src, c = (left, e) if e < 6 else (right, e - 42)
                    a = (6 * l + c) * 48 + (32 if r0 else 0)
                    buf[row:row + 6] = src[a:a + 16].astype(F32)[x0:x0 + 6]
                else:
                    buf[row:row + 6] = xs[l, e - 6].astype(F32)[x0:x0 + 6]
        to[0:HALO] = buf[...].astype(BF16)
        pick = (lanes((16, 48)) == rows((16, 48)) + r0).astype(BF16)
        a = dot_t(pick, wide[0].astype(BF16)[:, 0:48])
        b = dot_t(pick, wide[1].astype(BF16)[:, 0:48])
        zero = jnp.zeros((16, 80), F32)
        tail = jnp.concatenate([a, zero, b, zero, jnp.zeros((16, 256), F32)], axis=1)
        to[HALO:PAY] = jnp.where(rows((16, 512)) < 6, tail, 0.0).astype(BF16)


def inner_attention_body(x, land, pad, g1, wqkv, bias, ho, xg, *scratch):
    attend_setup(bias, scratch[0], scratch[9])

    @pl.loop(0, 4)
    def _(n):
        l, jc = n // 2, n % 2
        for c in range(12):
            v = x[l, 6 + jc * 12 + c].astype(F32)
            for i in range(3):
                xg.at[jc * 3 + i, pl.ds(pl.multiple_of(l * 144, 8), 144), :][12 * c:12 * c + 12] = v[6 + 12 * i:18 + 12 * i]

    gain = g1[...]
    land_b, pad_b = halves(land), halves(pad)

    def row_of(cells, w):
        lane = lanes((1, W)) % 144
        here = rows((36, W)) == 6 + (w // 3) * 12 + lane // 12
        pick = (rows((48, W)) == 6 + (w % 3) * 12 + lane % 12).astype(BF16)
        return jnp.sum(jnp.where(here, dot(cells, pick), 0.0), axis=0, keepdims=True)

    @pl.loop(0, 3)
    def _(n):
        pair((2 * n, 2 * n + 1), W, xg, lambda w: row_of(land_b, w), lambda w: row_of(pad_b, w) * NEG, gain, wqkv,
             lambda w: pl.multiple_of(w * W, 32), ho, scratch)


def inner_rest_body(ho, x, wout, g2, wup_hbm, wdown_hbm, out, edge, att, nat, wup, wdown, sems):
    copies = fetch(((wup_hbm, wup), (wdown_hbm, wdown)), sems)

    @pl.loop(0, 2)
    def _(n):
        h = ho[pl.ds(pl.multiple_of(n * 3 * W, 32), 3 * W), :]
        for c in range(2):
            r = dot(h, wout[:, c * 256:(c + 1) * 256])
            for i in range(3):
                att[n * 3 + i, :, c * 256:(c + 1) * 256] = r[i * W:(i + 1) * W]

    @pl.loop(0, 4)
    def _(n):
        l, jc = n // 2, n % 2
        for c in range(12):
            k = n * 12 + c
            for i in range(3):
                nat[k, 6 + 12 * i:18 + 12 * i] = att.at[jc * 3 + i, pl.ds(pl.multiple_of(l * 144, 8), 144), :][12 * c:12 * c + 12]
            nat[k] = nat[k] + x[l, 6 + jc * 12 + c].astype(F32)
            edge[k, 0] = nat[k, 0:8]
            edge[k, 1] = nat[k, 40:48]

    for c in copies:
        c.wait()
    gain = g2[...]

    @pl.loop(0, 2)
    def _(n):
        res = nat[pl.ds(n * 24, 24), 8:40, :].reshape(768, 512)
        out[pl.ds(n * 24, 24)] = feed_forward(res, gain, wup, wdown).reshape(24, 32, 512)


def edge_windows():
    tens = [(i, j) for i in (1, 2, 3) for j in (0, 3)] + [(i, j) for i in (0, 4) for j in (1, 2)]
    return tens + [(i, j) for i in (0, 4) for j in (0, 3)]


def pieces(i, j):
    runs = {0: ((6, 6), (0, 6)), 4: ((48, 6), (54, 6))}.get(i, ((12 * i, 12),))
    cols = {0: (range(6, 12), range(0, 6)), 3: (range(36, 42), range(42, 48))}.get(j, (range(12 * j, 12 * j + 12),))
    return [(l, e, f, n) for es in cols for f, n in runs for l in range(2) for e in es]


def cell_maps():
    e_of, f_of = [], []
    for i, j in edge_windows():
        e_of.append([e for l, e, f, n in pieces(i, j) for _ in range(n)])
        f_of.append([f + a for l, e, f, n in pieces(i, j) for a in range(n)])
    return np.array(e_of, np.int32)[:, None], np.array(f_of, np.int32)[:, None]


def border_body(flags, e_map, f_map, land, pad, x, left, right, up, down, inner_hbm, edge, g1, wqkv, bias, wout_hbm, g2, wup_hbm, wdown_hbm,
                out, xg, ho, att, nat_s, nat_i, wide, inner, wout, wup, wdown, sems, *scratch):
    copies = fetch(((inner_hbm, inner), (wout_hbm, wout), (wup_hbm, wup), (wdown_hbm, wdown)), sems)
    attend_setup(bias, scratch[0], scratch[9])
    wide_masks(land, pad, left, right, wide)
    wins = edge_windows()

    for w, (i, j) in enumerate(wins):
        row = 0
        for l, e, f, n in pieces(i, j):
            if f < 6 or f >= 54:
                a = 6 * (48 * l + e)
                lo = a // 16 * 16
                seg = (up if f < 6 else down)[lo:lo + 32].astype(F32)[a - lo:a - lo + 6]
            elif 6 <= e < 42:
                seg = x[l, e - 6].astype(F32)[f - 6:f - 6 + n]
            else:
                src, c = (left, e) if e < 6 else (right, e - 42)
                a = (6 * l + c) * 48
                seg = src[a:a + 48].astype(F32)[f - 6:f - 6 + n]
            xg[w, row:row + n, :] = seg
            row += n

    gain1 = g1[...]
    masks = [wide[n].astype(BF16)[:, 0:48] for n in range(2)]
    beyond = [jnp.concatenate([up[HALO:PAY, 128 * n:128 * n + 48], down[HALO:PAY, 128 * n:128 * n + 48]], axis=0) for n in range(2)]

    def row_of(n, w):
        e, f = e_map[w], f_map[w]
        pick_f = (rows((48, W)) == f - 6).astype(BF16)
        pick_e = (rows((48, W)) == e).astype(BF16)
        far = jnp.where(f < 6, f, f - 54 + 16)
        far = jnp.where((f < 6) | (f >= 54), far, 99)
        mid = jnp.sum(jnp.where(rows((48, W)) == e, dot(masks[n], pick_f), 0.0), axis=0, keepdims=True)
        return mid + jnp.sum(jnp.where(rows((32, W)) == far, dot(beyond[n], pick_e), 0.0), axis=0, keepdims=True)

    def blocked(w):
        f = f_map[w]
        over = ((f < 6) & (flags[0] > 0)) | ((f >= 54) & (flags[1] > 0))
        return jnp.where(over | (row_of(1, w) > 0.5), NEG, 0.0)

    for own, first, last in ((144, 0, 5), (72, 5, 7)):
        @pl.loop(first, last)
        def _(n):
            pair((2 * n, 2 * n + 1), own, xg, lambda w: row_of(0, w), blocked, gain1, wqkv,
                 lambda w: pl.multiple_of(w * 144, 16), ho, scratch)

    for c in copies:
        c.wait()

    @pl.loop(0, 2)
    def _(n):
        h = ho[pl.ds(pl.multiple_of(n * 1008, 16), 1008), :]
        for c in range(2):
            a = dot(h, wout[:, c * 256:(c + 1) * 256])
            for i in range(7):
                att[7 * n + i, :, c * 256:(c + 1) * 256] = a[144 * i:144 * i + 144]

    side = {c: s for s, c in enumerate(list(range(6)) + list(range(30, 36)))}
    for w, (i, j) in enumerate(wins):
        row = 0
        for l, e, f, n in pieces(i, j):
            if row == (144 if w < 10 else 72):
                break
            c, r = e - 6, f - 6
            seg = att[w, row:row + n, :]
            if c in side:
                nat_s[l * 12 + side[c], r:r + n, :] = seg
            elif r == 0:
                nat_i[l * 24 + c - 6, 0, 0:6, :] = seg
            else:
                nat_i[l * 24 + c - 6, 1, 2:8, :] = seg
            row += n
    gain2 = g2[...]

    @pl.loop(0, 2)
    def _(l):
        xs = jnp.concatenate([x[l, 0:6], x[l, 30:36]], axis=0).astype(F32)
        res = nat_s[pl.ds(12 * l, 12)] + xs
        y = feed_forward(res.reshape(576, 512), gain2, wup, wdown).reshape(12, 48, 512)
        out[l, 0:6] = y[0:6]
        out[l, 30:36] = y[6:12]

    @pl.loop(0, 2)
    def _(l):
        xs = x[l, 6:30].astype(F32)
        at = nat_i[pl.ds(24 * l, 24)]
        ed = edge[pl.ds(24 * l, 24)]
        low = jnp.where(rows((1, 8, 512)) < 6, at[:, 0] + xs[:, 0:8], ed[:, 0])
        high = jnp.where(rows((1, 8, 512)) >= 2, at[:, 1] + xs[:, 40:48], ed[:, 1])
        res = jnp.concatenate([low.reshape(192, 512), high.reshape(192, 512)], axis=0)
        y = feed_forward(res, gain2, wup, wdown).astype(F32)
        full = jnp.concatenate([y[0:192].reshape(24, 8, 512), inner[pl.ds(24 * l, 24)].astype(F32), y[192:384].reshape(24, 8, 512)], axis=1)
        out[l, 6:30] = full.astype(BF16)


VM = pl.BlockSpec(memory_space=pltpu.VMEM)
SM = pl.BlockSpec(memory_space=pltpu.SMEM)
HBM = pl.BlockSpec(memory_space=pl.ANY)


def params():
    return pltpu.CompilerParams(vmem_limit_bytes=60 * MB)


def cost(flops, nbytes):
    return pl.CostEstimate(flops=flops, bytes_accessed=nbytes, transcendentals=0)


def pack_lon(xt, land, pad):
    strip = jax.ShapeDtypeStruct((PAY, 512), BF16)
    return pl.pallas_call(
        pack_lon_body, grid=(1,), out_shape=[strip] * 2,
        in_specs=[pl.BlockSpec((2, 6, 48, 512), lambda i: (0, 0, 0, 0)), pl.BlockSpec((2, 6, 48, 512), lambda i: (0, 5, 0, 0)), VM, VM],
        out_specs=[VM] * 2, compiler_params=pltpu.CompilerParams(vmem_limit_bytes=16 * MB), cost_estimate=cost(1, 2 * MB))(xt, xt, land, pad)


def pack_lat(xt, left, right, land, pad):
    strip = jax.ShapeDtypeStruct((PAY, 512), BF16)
    return pl.pallas_call(
        pack_lat_body, grid=(1,), out_shape=[strip] * 2,
        in_specs=[pl.BlockSpec((2, 36, 16, 512), lambda i: (0, 0, 0, 0)), pl.BlockSpec((2, 36, 16, 512), lambda i: (0, 0, 2, 0)), VM, VM, VM, VM],
        out_specs=[VM] * 2, scratch_shapes=[pltpu.VMEM((HALO, 512), F32), pltpu.VMEM((2, 48, 128), F32)],
        compiler_params=pltpu.CompilerParams(vmem_limit_bytes=24 * MB), cost_estimate=cost(1, 4 * MB))(xt, xt, left, right, land, pad)


def inner_attention(xt, land, pad, g1, wqkv, bias):
    return pl.pallas_call(
        inner_attention_body, out_shape=jax.ShapeDtypeStruct((6 * W, 512), BF16),
        in_specs=[VM] * 5 + [SM], out_specs=VM,
        scratch_shapes=[pltpu.VMEM((6, W, 512), F32)] + attend_scratch(W),
        compiler_params=params(), cost_estimate=cost(22 * 10**9, 8 * MB))(xt, land, pad, g1, wqkv, bias)


def inner_rest(ho, xt, wout, g2, wup, wdown):
    return pl.pallas_call(
        inner_rest_body, out_shape=[jax.ShapeDtypeStruct((48, 32, 512), BF16), jax.ShapeDtypeStruct((48, 2, 8, 512), F32)],
        in_specs=[VM] * 4 + [HBM] * 2, out_specs=[VM] * 2,
        scratch_shapes=[pltpu.VMEM((6, W, 512), F32), pltpu.VMEM((48, 48, 512), F32), pltpu.VMEM((512, 2048), BF16), pltpu.VMEM((2048, 512), BF16),
                        pltpu.SemaphoreType.DMA((2,))],
        compiler_params=params(), cost_estimate=cost(16 * 10**9, 10 * MB))(ho, xt, wout, g2, wup, wdown)


def border(flags, land, pad, xt, left, right, up, down, inner, edge, g1, wqkv, bias, wout, g2, wup, wdown):
    e_map, f_map = cell_maps()
    return pl.pallas_call(
        border_body, out_shape=jax.ShapeDtypeStruct((2, 36, 48, 512), BF16),
        in_specs=[SM] + [VM] * 9 + [HBM, VM, VM, VM, SM, HBM, VM, HBM, HBM], out_specs=VM,
        scratch_shapes=[
            pltpu.VMEM((14, W, 512), F32),
            pltpu.VMEM((14 * 144, 512), BF16),
            pltpu.VMEM((14, 144, 512), F32),
            pltpu.VMEM((24, 48, 512), F32),
            pltpu.VMEM((48, 2, 8, 512), F32),
            pltpu.VMEM((2, 48, 128), F32),
            pltpu.VMEM((48, 32, 512), BF16),
            pltpu.VMEM((512, 512), BF16),
            pltpu.VMEM((512, 2048), BF16),
            pltpu.VMEM((2048, 512), BF16),
            pltpu.SemaphoreType.DMA((4,)),
        ] + attend_scratch(144),
        compiler_params=params(), cost_estimate=cost(40 * 10**9, 20 * MB))(
            flags, jnp.asarray(e_map), jnp.asarray(f_map), land, pad, xt, left, right, up, down, inner, edge, g1, wqkv, bias, wout, g2, wup, wdown)


def from_behind(value, axis, by):
    devices = lax.axis_size(axis)
    return lax.ppermute(value, axis, [(i, (i + by) % devices) for i in range(devices)])


def on_device(latent_field, land_mask, padded, norm1_gain, qkv_weight, land_bias, out_weight, norm2_gain, up_weight, down_weight):
    xt = latent_field.transpose(0, 2, 1, 3)
    land, pad = land_mask.T, padded.T
    g1, g2 = norm1_gain.reshape(1, 512), norm2_gain.reshape(1, 512)
    lat = lax.axis_index("lat")
    flags = jnp.stack([(lat == 0).astype(jnp.int32), (lat == lax.axis_size("lat") - 1).astype(jnp.int32)])
    to_right, to_left = pack_lon(xt, land, pad)
    left, right = from_behind(to_right, "lon", 1), from_behind(to_left, "lon", -1)
    ho = inner_attention(xt, land, pad, g1, qkv_weight, land_bias)
    ho, left, right = lax.optimization_barrier((ho, left, right))
    to_down, to_up = pack_lat(xt, left, right, land, pad)
    up, down = from_behind(to_down, "lat", 1), from_behind(to_up, "lat", -1)
    inner, edge = inner_rest(ho, xt, out_weight, g2, up_weight, down_weight)
    y = border(flags, land, pad, xt, left, right, up, down, inner, edge, g1, qkv_weight, land_bias, out_weight, g2, up_weight, down_weight)
    return y.transpose(0, 2, 1, 3)


def solution(mesh):
    spec = P(None, "lat", "lon", None)
    placed = (spec, P("lat", "lon"), P("lat", "lon")) + (P(),) * 7
    return jax.shard_map(on_device, mesh=mesh, in_specs=placed, out_specs=spec, check_vma=False)
```

```python
import functools
import math

import jax
import jax.numpy as jnp
import numpy as np
from jax import lax
from jax.experimental import pallas as pl
from jax.experimental.pallas import tpu as pltpu
from jax.sharding import PartitionSpec as P

F32, BF16 = jnp.float32, jnp.bfloat16
LOG2E = math.log2(math.e)
SCALE = LOG2E / math.sqrt(32.0)
W = 288
HALO = 576
PAY = HALO + 16
NEG = -1e30
MB = 1024 * 1024
LIMIT = 65200 * 1024


def dot(a, b):
    return lax.dot_general(a, b, (((1,), (0,)), ((), ())), preferred_element_type=F32)


def dot_t(a, b):
    return lax.dot_general(a, b, (((1,), (1,)), ((), ())), preferred_element_type=F32)


def norm(x, g):
    c = x - jnp.mean(x, axis=-1, keepdims=True)
    s = jnp.mean(c * c, axis=-1, keepdims=True)
    return (c * lax.rsqrt(s + 1e-5) * g).astype(BF16)


def lanes(shape):
    return lax.broadcasted_iota(jnp.int32, shape, len(shape) - 1)


def rows(shape):
    return lax.broadcasted_iota(jnp.int32, shape, len(shape) - 2)


def gelu(x):
    return 0.5 * x * (1.0 + lax.erf(x * (1 / math.sqrt(2.0))))


def halves(cells):
    return cells[...].astype(F32).astype(BF16)


def operand_scratch(nq):
    return [
        pltpu.VMEM((2, 4, 4 * nq, 128), BF16),
        pltpu.VMEM((2, nq, 512), BF16),
        pltpu.VMEM((2, W, 512), BF16),
        pltpu.VMEM((2, 4, 1152, 128), BF16),
        pltpu.VMEM((2, 4 * nq, 128), BF16),
        pltpu.VMEM((2, W, 128), F32),
        pltpu.VMEM((2, nq, 256), F32),
        pltpu.VMEM((2, nq, 128), F32),
    ]


def attend_scratch(nq):
    return [
        pltpu.VMEM((8, 128), F32),
        pltpu.VMEM((1152, 128), BF16),
        *[pltpu.VMEM((4 * nq, 256), F32)] * 2,
        *[pltpu.VMEM((nq, 128), F32)] * 2,
        *[pltpu.VMEM((nq, 1152), BF16)] * 2,
    ]


def attend_setup(bias_ref, brow, ones):
    at = lanes((1, 128))
    for g in range(4):
        line = jnp.zeros((1, 128), F32)
        for h in range(4):
            full = jnp.full((1, 128), bias_ref[4 * g + h] * LOG2E, F32)
            hi = full.astype(BF16).astype(F32)
            mid = (full - hi).astype(BF16).astype(F32)
            for n, part in enumerate((hi, mid, full - hi - mid)):
                line = jnp.where(at == 3 * h + n, part, line)
        brow[g:g + 1] = line
    for h in range(4):
        hm = (at // 32 == h).astype(BF16)
        ones[256 * h:256 * h + 256] = jnp.broadcast_to(hm, (256, 128))
        ones[1024 + 32 * h:1056 + 32 * h] = jnp.broadcast_to(hm, (32, 128))


def head_lanes():
    spot = lanes((1, 128))
    return spot, [(spot // 32 == h).astype(BF16) for h in range(4)], [(spot // 3 == h).astype(BF16) for h in range(4)]


def project(ws, tokens, land_row, blocked_row, gain, wqkv, operands):
    qst, qpl, kpl, vst, lqx, lk, mk, mkt = operands
    nq = qpl.shape[1]
    spot, hms, threes = head_lanes()
    xn = jnp.concatenate([norm(tokens[w], gain) for w in ws], axis=0)
    xq = xn if nq == W else jnp.concatenate([xn[0:nq], xn[W:W + nq]], axis=0)
    for c in range(6):
        cols = slice(c * 256, (c + 1) * 256)
        if c < 2:
            r = (dot(xq, wqkv[:, cols]) * SCALE).astype(BF16)
            for a in range(2):
                ra = r[a * nq:(a + 1) * nq]
                qpl[a, :, cols] = ra
                for gl in range(2):
                    for h in range(4):
                        qst[a, 2 * c + gl, h * nq:(h + 1) * nq] = ra[:, gl * 128:(gl + 1) * 128] * hms[h]
        else:
            r = dot(xn, wqkv[:, cols]).astype(BF16)
            for a in range(2):
                ra = r[a * W:(a + 1) * W]
                if c < 4:
                    kpl[a, :, (c - 2) * 256:(c - 1) * 256] = ra
                    continue
                for gl in range(2):
                    g = 2 * (c - 4) + gl
                    for h in range(4):
                        vm = ra[:, gl * 128:(gl + 1) * 128] * hms[h]
                        vst[a, g, 256 * h:256 * h + 256] = vm[0:256]
                        vst[a, g, 1024 + 32 * h:1056 + 32 * h] = vm[256:288]
    eye = rows((W, W)) == lanes((W, W))
    for a, w in enumerate(ws):
        land = jnp.broadcast_to(jnp.sum(jnp.where(eye, land_row(w), 0.0), axis=1, keepdims=True), (W, 128))
        lk[a] = land
        lq = land[0:nq].astype(BF16)
        for h in range(4):
            lqx[a, h * nq:(h + 1) * nq] = lq * threes[h]
        mm = jnp.where(eye[0:nq], 0.0, blocked_row(w))
        mk[a] = mm[:, 0:256]
        mkt[a] = jnp.concatenate([mm[:, 256:288]] * 4, axis=1)


def attend(ws, own, out_row, ho, common, operands):
    brow, ones, s0, s1, t0, t1, p0, p1 = common
    qst, qpl, kpl, vst, lqx, lk, mk, mkt = operands
    nq = qpl.shape[1]
    spot, hms, threes = head_lanes()
    ss, ts, ps = (s0, s1), (t0, t1), (p0, p1)

    def q_step(n):
        a, g, b = n // 4, n % 4, n % 2
        k = kpl[a, :, g * 128:(g + 1) * 128]
        kx = (lk[a] * brow[g:g + 1]).astype(BF16)
        ss[b][...] = dot_t(jnp.concatenate([qst[a, g], lqx[a]], axis=1), jnp.concatenate([k[0:256], kx[0:256]], axis=1))
        kt = jnp.concatenate([
            jnp.concatenate([k[256:288] * hms[h] for h in range(4)], axis=0),
            jnp.concatenate([kx[256:288] * threes[h] for h in range(4)], axis=0)], axis=1)
        lq = lk[a, 0:nq].astype(BF16)
        ts[b][...] = dot_t(jnp.concatenate([qpl[a, :, g * 128:(g + 1) * 128], lq], axis=1), kt)

    def s_step(n):
        a, b = n // 4, n % 2
        for r in range(0, own, 16):
            at = slice(r, min(r + 16, own))
            size = at.stop - r
            t = ts[b][at] + mkt[a, at]
            mask = mk[a, at]
            tops = []
            for h in range(4):
                s = ss[b][h * nq + r:h * nq + r + size] + mask
                m = jnp.maximum(jnp.maximum(s[:, :128], s[:, 128:]), jnp.where(spot // 32 == h, t, -3e38))
                m = jnp.max(m, axis=-1, keepdims=True)
                ps[b][at, h * 256:(h + 1) * 256] = jnp.exp2(s - m).astype(BF16)
                tops.append(m)
            top = jnp.where(spot < 32, tops[0], jnp.where(spot < 64, tops[1], jnp.where(spot < 96, tops[2], tops[3])))
            ps[b][at, 1024:1152] = jnp.exp2(t - top).astype(BF16)

    def v_step(n):
        a, g, b = n // 4, n % 4, n % 2
        o = dot(ps[b][0:own], jnp.concatenate([vst[a, g], ones[...]], axis=1))
        ho[pl.ds(out_row(ws[a]), own), g * 128:(g + 1) * 128] = (o[:, :128] / o[:, 128:]).astype(BF16)

    for n in range(10):
        if n < 8:
            q_step(n)
        if 1 <= n < 9:
            s_step(n - 1)
        if n >= 2:
            v_step(n - 2)


def feed_forward(res, gain, wup, wdown):
    xn = norm(res, gain)
    acc = res
    for c in range(4):
        hidden = gelu(dot(xn, wup[:, c * 512:(c + 1) * 512])).astype(BF16)
        acc = acc + dot(hidden, wdown[c * 512:(c + 1) * 512, :])
    return acc.astype(BF16)


def fetch(pairs, sems):
    copies = [pltpu.make_async_copy(src, dst, sems.at[n]) for n, (src, dst) in enumerate(pairs)]
    for c in copies:
        c.start()
    return copies


def pack_lon_body(first, last, land, pad, to_right, to_left):
    for strip, c0, to in ((last, 30, to_right), (first, 0, to_left)):
        to[0:HALO] = strip[...].reshape(HALO, 512)
        zero = jnp.zeros((10, 128), F32)
        a = jnp.concatenate([land[c0:c0 + 6].astype(F32), jnp.zeros((6, 80), F32)], axis=1)
        b = jnp.concatenate([pad[c0:c0 + 6].astype(F32), jnp.zeros((6, 80), F32)], axis=1)
        a = jnp.concatenate([a, zero], axis=0)
        b = jnp.concatenate([b, zero], axis=0)
        to[HALO:PAY] = jnp.concatenate([a, b, jnp.zeros((16, 256), F32)], axis=1).astype(BF16)


def wide_masks(land, pad, left, right, wide):
    l, r = left[HALO:PAY].astype(F32), right[HALO:PAY].astype(F32)
    for n, own in enumerate((land, pad)):
        wide[n, 0:6, 0:48] = l[0:6, 128 * n:128 * n + 48]
        wide[n, 6:42, 0:48] = own[...].astype(F32)
        wide[n, 42:48, 0:48] = r[0:6, 128 * n:128 * n + 48]


def pack_lat_body(x_low, x_high, left, right, land, pad, to_down, to_up, buf, wide):
    wide_masks(land, pad, left, right, wide)
    for to, xs, r0 in ((to_down, x_high, 42), (to_up, x_low, 0)):
        x0 = 10 if r0 else 0
        for l in range(2):
            for e in range(48):
                row = 6 * (48 * l + e)
                if e < 6 or e >= 42:
                    src, c = (left, e) if e < 6 else (right, e - 42)
                    a = (6 * l + c) * 48 + (32 if r0 else 0)
                    buf[row:row + 6] = src[a:a + 16].astype(F32)[x0:x0 + 6]
                else:
                    buf[row:row + 6] = xs[l, e - 6].astype(F32)[x0:x0 + 6]
        to[0:HALO] = buf[...].astype(BF16)
        pick = (lanes((16, 48)) == rows((16, 48)) + r0).astype(BF16)
        a = dot_t(pick, wide[0].astype(BF16)[:, 0:48])
        b = dot_t(pick, wide[1].astype(BF16)[:, 0:48])
        zero = jnp.zeros((16, 80), F32)
        tail = jnp.concatenate([a, zero, b, zero, jnp.zeros((16, 256), F32)], axis=1)
        to[HALO:PAY] = jnp.where(rows((16, 512)) < 6, tail, 0.0).astype(BF16)


def inner_attention_body(x_hbm, land, pad, g1, wqkv_hbm, bias, ho, xg, x, wqkv, sems, *scratch):
    parts = [(l, jc) for jc in range(2) for l in range(2)]
    copies = fetch([(x_hbm.at[l, pl.ds(6 + 12 * jc, 12)], x.at[n]) for n, (l, jc) in enumerate(parts)] + [(wqkv_hbm, wqkv)], sems)
    common, operands = scratch[:8], scratch[8:]
    attend_setup(bias, common[0], common[1])
    for n, (l, jc) in enumerate(parts):
        copies[n].wait()
        for c in range(12):
            v = x[n, c].astype(F32)
            for i in range(3):
                xg[jc * 3 + i, l * 144 + 12 * c:l * 144 + 12 * c + 12, :] = v[6 + 12 * i:18 + 12 * i]
    copies[4].wait()

    gain = g1[...]
    land_b, pad_b = halves(land), halves(pad)

    def row_of(cells, w):
        lane = lanes((1, W)) % 144
        here = rows((36, W)) == 6 + (w // 3) * 12 + lane // 12
        pick = (rows((48, W)) == 6 + (w % 3) * 12 + lane % 12).astype(BF16)
        return jnp.sum(jnp.where(here, dot(cells, pick), 0.0), axis=0, keepdims=True)

    @pl.loop(0, 3)
    def _(n):
        ws = (2 * n, 2 * n + 1)
        project(ws, xg, lambda w: row_of(land_b, w), lambda w: row_of(pad_b, w) * NEG, gain, wqkv, operands)
        attend(ws, W, lambda w: pl.multiple_of(w * W, 32), ho, common, operands)


def inner_rest_body(ho, x, wout, g2, wup_hbm, wdown_hbm, out, edge, att, nat, wup, wdown, sems):
    copies = fetch(((wup_hbm, wup), (wdown_hbm, wdown)), sems)

    @pl.loop(0, 2)
    def _(n):
        h = ho[pl.ds(pl.multiple_of(n * 3 * W, 32), 3 * W), :]
        for c in range(2):
            r = dot(h, wout[:, c * 256:(c + 1) * 256])
            for i in range(3):
                att[n * 3 + i, :, c * 256:(c + 1) * 256] = r[i * W:(i + 1) * W]

    @pl.loop(0, 4)
    def _(n):
        l, jc = n // 2, n % 2
        for c in range(12):
            k = n * 12 + c
            for i in range(3):
                nat[k, 6 + 12 * i:18 + 12 * i] = att.at[jc * 3 + i, pl.ds(pl.multiple_of(l * 144, 8), 144), :][12 * c:12 * c + 12]
            nat[k] = nat[k] + x[l, 6 + jc * 12 + c].astype(F32)
            edge[k, 0] = nat[k, 0:8]
            edge[k, 1] = nat[k, 40:48]

    for c in copies:
        c.wait()
    gain = g2[...]

    @pl.loop(0, 2)
    def _(n):
        res = nat[pl.ds(n * 24, 24), 8:40, :].reshape(768, 512)
        out[pl.ds(n * 24, 24)] = feed_forward(res, gain, wup, wdown).reshape(24, 32, 512)


def edge_windows():
    tens = [(i, j) for i in (1, 2, 3) for j in (0, 3)] + [(i, j) for i in (0, 4) for j in (1, 2)]
    return tens + [(i, j) for i in (0, 4) for j in (0, 3)]


def pieces(i, j):
    runs = {0: ((6, 6), (0, 6)), 4: ((48, 6), (54, 6))}.get(i, ((12 * i, 12),))
    cols = {0: (range(6, 12), range(0, 6)), 3: (range(36, 42), range(42, 48))}.get(j, (range(12 * j, 12 * j + 12),))
    return [(l, e, f, n) for es in cols for f, n in runs for l in range(2) for e in es]


def cell_maps():
    e_of, f_of = [], []
    for i, j in edge_windows():
        e_of.append([e for l, e, f, n in pieces(i, j) for _ in range(n)])
        f_of.append([f + a for l, e, f, n in pieces(i, j) for a in range(n)])
    return np.array(e_of, np.int32)[:, None], np.array(f_of, np.int32)[:, None]


def border_body(e_map, f_map, land, pad, x_hbm, left_hbm, right_hbm, up_hbm, down_hbm, inner_hbm, edge_hbm, g1, wqkv_hbm, bias, wout_hbm, g2, wup_hbm,
                wdown_hbm, out_hbm, x, left, right, up, down, edge, wqkv, out, xg, ho, att, nat_s, nat_i, wide, inner, wout, wup, wdown, sems, *scratch):
    sides = (slice(0, 6), slice(30, 36))
    copies = fetch([(x_hbm.at[:, pl.ds(0, 6)], x.at[:, pl.ds(0, 6)]), (x_hbm.at[:, pl.ds(30, 6)], x.at[:, pl.ds(30, 6)]),
                    (left_hbm, left), (right_hbm, right), (wqkv_hbm, wqkv), (up_hbm, up), (down_hbm, down),
                    (x_hbm.at[:, pl.ds(6, 24)], x.at[:, pl.ds(6, 24)]), (wout_hbm, wout), (edge_hbm, edge), (inner_hbm, inner),
                    (wup_hbm, wup), (wdown_hbm, wdown)], sems)
    common, operands = scratch[:8], (scratch[8:16], scratch[16:24])
    attend_setup(bias, common[0], common[1])
    lat = lax.axis_index("lat")
    first_row, last_row = lat == 0, lat == lax.axis_size("lat") - 1
    for c in copies[:4]:
        c.wait()
    wide_masks(land, pad, left, right, wide)
    wins = edge_windows()
    gain1 = g1[...]

    def gather(w):
        i, j = wins[w]
        row = 0
        for l, e, f, n in pieces(i, j):
            if f < 6 or f >= 54:
                a = 6 * (48 * l + e)
                lo = a // 16 * 16
                seg = (up if f < 6 else down)[lo:lo + 32].astype(F32)[a - lo:a - lo + 6]
            elif 6 <= e < 42:
                seg = x[l, e - 6].astype(F32)[f - 6:f - 6 + n]
            else:
                src, c = (left, e) if e < 6 else (right, e - 42)
                a = (6 * l + c) * 48
                seg = src[a:a + 48].astype(F32)[f - 6:f - 6 + n]
            xg[w, row:row + n, :] = seg
            row += n

    masks = [wide[n].astype(BF16)[:, 0:48] for n in range(2)]

    def row_of(n, w):
        e, f = e_map[w], f_map[w]
        pick_f = (rows((48, W)) == f - 6).astype(BF16)
        pick_e = (rows((48, W)) == e).astype(BF16)
        far = jnp.where(f < 6, f, f - 54 + 16)
        far = jnp.where((f < 6) | (f >= 54), far, 99)
        mid = jnp.sum(jnp.where(rows((48, W)) == e, dot(masks[n], pick_f), 0.0), axis=0, keepdims=True)
        beyond = jnp.concatenate([up[HALO:PAY, 128 * n:128 * n + 48], down[HALO:PAY, 128 * n:128 * n + 48]], axis=0)
        return mid + jnp.sum(jnp.where(rows((32, W)) == far, dot(beyond, pick_e), 0.0), axis=0, keepdims=True)

    def blocked(w):
        f = f_map[w]
        over = ((f < 6) & first_row) | ((f >= 54) & last_row)
        return jnp.where(over | (row_of(1, w) > 0.5), NEG, 0.0)

    def operands_of(n):
        project((2 * n, 2 * n + 1), xg, lambda w: row_of(0, w), blocked, gain1, wqkv, operands[n % 2])

    for w in range(6):
        gather(w)
    for c in copies[4:8]:
        c.wait()
    operands_of(0)
    for n in range(7):
        if n == 0:
            for w in range(6, 14):
                gather(w)
        if n < 6:
            operands_of(n + 1)
        attend((2 * n, 2 * n + 1), 144 if n < 5 else 72, lambda w: w * 144, ho, common, operands[n % 2])

    for c in copies[8:]:
        c.wait()

    @pl.loop(0, 2)
    def _(n):
        h = ho[pl.ds(pl.multiple_of(n * 1008, 16), 1008), :]
        for c in range(2):
            a = dot(h, wout[:, c * 256:(c + 1) * 256])
            for i in range(7):
                att[7 * n + i, :, c * 256:(c + 1) * 256] = a[144 * i:144 * i + 144]

    side = {c: s for s, c in enumerate(list(range(6)) + list(range(30, 36)))}
    for w, (i, j) in enumerate(wins):
        row = 0
        for l, e, f, n in pieces(i, j):
            if row == (144 if w < 10 else 72):
                break
            c, r = e - 6, f - 6
            seg = att[w, row:row + n, :]
            if c in side:
                nat_s[l * 12 + side[c], r:r + n, :] = seg
            elif r == 0:
                nat_i[l * 24 + c - 6, 0, 0:6, :] = seg
            else:
                nat_i[l * 24 + c - 6, 1, 2:8, :] = seg
            row += n
    gain2 = g2[...]
    xs = jnp.concatenate([x[l, at] for l in range(2) for at in sides], axis=0).astype(F32)
    y = feed_forward((nat_s[...] + xs).reshape(1152, 512), gain2, wup, wdown).reshape(24, 48, 512)
    sent = []
    for n, (l, at) in enumerate([(l, at) for l in range(2) for at in sides]):
        out[l, at] = y[6 * n:6 * n + 6]
        sent.append(pltpu.make_async_copy(out.at[l, pl.ds(at.start, 6)], out_hbm.at[l, pl.ds(at.start, 6)], sems.at[n]))
        sent[-1].start()
    xs = x[:, 6:30].astype(F32).reshape(48, 48, 512)
    low = jnp.where(rows((1, 8, 512)) < 6, nat_i[:, 0] + xs[:, 0:8], edge[:, 0])
    high = jnp.where(rows((1, 8, 512)) >= 2, nat_i[:, 1] + xs[:, 40:48], edge[:, 1])
    res = jnp.concatenate([low.reshape(384, 512), high.reshape(384, 512)], axis=0)
    y = feed_forward(res, gain2, wup, wdown).astype(F32)
    low, high = y[0:384].reshape(48, 8, 512), y[384:768].reshape(48, 8, 512)
    for l in range(2):
        at = slice(24 * l, 24 * l + 24)
        out[l, 6:30] = jnp.concatenate([low[at], inner[at].astype(F32), high[at]], axis=1).astype(BF16)
        sent.append(pltpu.make_async_copy(out.at[l, pl.ds(6, 24)], out_hbm.at[l, pl.ds(6, 24)], sems.at[4 + l]))
        sent[-1].start()
    for c in sent:
        c.wait()


VM = pl.BlockSpec(memory_space=pltpu.VMEM)
SM = pl.BlockSpec(memory_space=pltpu.SMEM)
HBM = pl.BlockSpec(memory_space=pl.ANY)


def params():
    return pltpu.CompilerParams(vmem_limit_bytes=LIMIT)


def cost(flops, nbytes):
    return pl.CostEstimate(flops=flops, bytes_accessed=nbytes, transcendentals=0)


def pack_lon(xt, land, pad):
    strip = jax.ShapeDtypeStruct((PAY, 512), BF16)
    return pl.pallas_call(
        pack_lon_body, grid=(1,), out_shape=[strip] * 2,
        in_specs=[pl.BlockSpec((2, 6, 48, 512), lambda i: (0, 0, 0, 0)), pl.BlockSpec((2, 6, 48, 512), lambda i: (0, 5, 0, 0)), VM, VM],
        out_specs=[VM] * 2, compiler_params=pltpu.CompilerParams(vmem_limit_bytes=LIMIT), cost_estimate=cost(1, 2 * MB))(xt, xt, land, pad)


def pack_lat(xt, left, right, land, pad):
    strip = jax.ShapeDtypeStruct((PAY, 512), BF16)
    return pl.pallas_call(
        pack_lat_body, grid=(1,), out_shape=[strip] * 2,
        in_specs=[pl.BlockSpec((2, 36, 16, 512), lambda i: (0, 0, 0, 0)), pl.BlockSpec((2, 36, 16, 512), lambda i: (0, 0, 2, 0)), VM, VM, VM, VM],
        out_specs=[VM] * 2, scratch_shapes=[pltpu.VMEM((HALO, 512), F32), pltpu.VMEM((2, 48, 128), F32)],
        compiler_params=pltpu.CompilerParams(vmem_limit_bytes=LIMIT), cost_estimate=cost(1, 4 * MB))(xt, xt, left, right, land, pad)


def inner_attention(xt, land, pad, g1, wqkv, bias):
    return pl.pallas_call(
        inner_attention_body, out_shape=jax.ShapeDtypeStruct((6 * W, 512), BF16),
        in_specs=[HBM, VM, VM, VM, HBM, SM], out_specs=VM,
        scratch_shapes=[pltpu.VMEM((6, W, 512), F32), pltpu.VMEM((4, 12, 48, 512), BF16), pltpu.VMEM((512, 1536), BF16),
                        pltpu.SemaphoreType.DMA((5,))] + attend_scratch(W) + operand_scratch(W),
        compiler_params=params(), cost_estimate=cost(22 * 10**9, 8 * MB))(xt, land, pad, g1, wqkv, bias)


def inner_rest(ho, xt, wout, g2, wup, wdown):
    return pl.pallas_call(
        inner_rest_body, out_shape=[jax.ShapeDtypeStruct((48, 32, 512), BF16), jax.ShapeDtypeStruct((48, 2, 8, 512), F32)],
        in_specs=[VM] * 4 + [HBM] * 2, out_specs=[VM] * 2,
        scratch_shapes=[pltpu.VMEM((6, W, 512), F32), pltpu.VMEM((48, 48, 512), F32), pltpu.VMEM((512, 2048), BF16), pltpu.VMEM((2048, 512), BF16),
                        pltpu.SemaphoreType.DMA((2,))],
        compiler_params=params(), cost_estimate=cost(16 * 10**9, 10 * MB))(ho, xt, wout, g2, wup, wdown)


def border(land, pad, xt, left, right, up, down, inner, edge, g1, wqkv, bias, wout, g2, wup, wdown):
    e_map, f_map = cell_maps()
    return pl.pallas_call(
        border_body, out_shape=jax.ShapeDtypeStruct((2, 36, 48, 512), BF16),
        in_specs=[VM] * 4 + [HBM] * 7 + [VM, HBM, SM, HBM, VM, HBM, HBM], out_specs=HBM,
        scratch_shapes=[
            pltpu.VMEM((2, 36, 48, 512), BF16),
            *[pltpu.VMEM((PAY, 512), BF16)] * 4,
            pltpu.VMEM((48, 2, 8, 512), F32),
            pltpu.VMEM((512, 1536), BF16),
            pltpu.VMEM((2, 36, 48, 512), BF16),
            pltpu.VMEM((14, W, 512), F32),
            pltpu.VMEM((14 * 144, 512), BF16),
            pltpu.VMEM((14, 144, 512), F32),
            pltpu.VMEM((24, 48, 512), F32),
            pltpu.VMEM((48, 2, 8, 512), F32),
            pltpu.VMEM((2, 48, 128), F32),
            pltpu.VMEM((48, 32, 512), BF16),
            pltpu.VMEM((512, 512), BF16),
            pltpu.VMEM((512, 2048), BF16),
            pltpu.VMEM((2048, 512), BF16),
            pltpu.SemaphoreType.DMA((13,)),
        ] + attend_scratch(144) + operand_scratch(144) * 2,
        compiler_params=params(), cost_estimate=cost(40 * 10**9, 20 * MB))(
            jnp.asarray(e_map), jnp.asarray(f_map), land, pad, xt, left, right, up, down, inner, edge, g1, wqkv, bias, wout, g2, wup, wdown)


def from_behind(value, axis, by):
    devices = lax.axis_size(axis)
    return lax.ppermute(value, axis, [(i, (i + by) % devices) for i in range(devices)])


def on_device(latent_field, land_mask, padded, norm1_gain, qkv_weight, land_bias, out_weight, norm2_gain, up_weight, down_weight):
    xt = latent_field.transpose(0, 2, 1, 3)
    land, pad = land_mask.T, padded.T
    g1, g2 = norm1_gain.reshape(1, 512), norm2_gain.reshape(1, 512)
    to_right, to_left = pack_lon(xt, land, pad)
    left, right = from_behind(to_right, "lon", 1), from_behind(to_left, "lon", -1)
    ho = inner_attention(xt, land, pad, g1, qkv_weight, land_bias)
    ho, left, right = lax.optimization_barrier((ho, left, right))
    to_down, to_up = pack_lat(xt, left, right, land, pad)
    up, down = from_behind(to_down, "lat", 1), from_behind(to_up, "lat", -1)
    inner, edge = inner_rest(ho, xt, out_weight, g2, up_weight, down_weight)
    y = border(land, pad, xt, left, right, up, down, inner, edge, g1, qkv_weight, land_bias, out_weight, g2, up_weight, down_weight)
    return y.transpose(0, 2, 1, 3)


def solution(mesh):
    spec = P(None, "lat", "lon", None)
    placed = (spec, P("lat", "lon"), P("lat", "lon")) + (P(),) * 7
    return jax.shard_map(on_device, mesh=mesh, in_specs=placed, out_specs=spec, check_vma=False)
```

```python
import functools
import math

import jax
import jax.numpy as jnp
import numpy as np
from jax import lax
from jax.experimental import pallas as pl
from jax.experimental.pallas import tpu as pltpu
from jax.sharding import PartitionSpec as P

F32, BF16 = jnp.float32, jnp.bfloat16
LOG2E = math.log2(math.e)
SCALE = LOG2E / math.sqrt(32.0)
W = 288
HALO = 576
PAY = HALO + 16
NEG = -1e30
MB = 1024 * 1024
LIMIT = 65200 * 1024


def dot(a, b):
    return lax.dot_general(a, b, (((1,), (0,)), ((), ())), preferred_element_type=F32)


def dot_t(a, b):
    return lax.dot_general(a, b, (((1,), (1,)), ((), ())), preferred_element_type=F32)


def norm(x, g):
    c = x - jnp.mean(x, axis=-1, keepdims=True)
    s = jnp.mean(c * c, axis=-1, keepdims=True)
    return (c * lax.rsqrt(s + 1e-5) * g).astype(BF16)


def lanes(shape):
    return lax.broadcasted_iota(jnp.int32, shape, len(shape) - 1)


def rows(shape):
    return lax.broadcasted_iota(jnp.int32, shape, len(shape) - 2)


def gelu(x):
    return 0.5 * x * (1.0 + lax.erf(x * (1 / math.sqrt(2.0))))


def halves(cells):
    return cells[...].astype(F32).astype(BF16)


def operand_scratch(nq):
    return [
        pltpu.VMEM((2, 4, 4 * nq, 128), BF16),
        pltpu.VMEM((2, nq, 512), BF16),
        pltpu.VMEM((2, W, 512), BF16),
        pltpu.VMEM((2, 4, 1152, 128), BF16),
        pltpu.VMEM((2, 4 * nq, 128), BF16),
        pltpu.VMEM((2, W, 128), F32),
        pltpu.VMEM((2, nq, 256), F32),
        pltpu.VMEM((2, nq, 128), F32),
    ]


def attend_scratch(nq):
    return [
        pltpu.VMEM((8, 128), F32),
        pltpu.VMEM((1152, 128), BF16),
        *[pltpu.VMEM((4 * nq, 256), F32)] * 2,
        *[pltpu.VMEM((nq, 128), F32)] * 2,
        *[pltpu.VMEM((nq, 1152), BF16)] * 2,
    ]


def attend_setup(bias_ref, brow, ones):
    at = lanes((1, 128))
    for g in range(4):
        line = jnp.zeros((1, 128), F32)
        for h in range(4):
            full = jnp.full((1, 128), bias_ref[4 * g + h] * LOG2E, F32)
            hi = full.astype(BF16).astype(F32)
            mid = (full - hi).astype(BF16).astype(F32)
            for n, part in enumerate((hi, mid, full - hi - mid)):
                line = jnp.where(at == 3 * h + n, part, line)
        brow[g:g + 1] = line
    for h in range(4):
        hm = (at // 32 == h).astype(BF16)
        ones[256 * h:256 * h + 256] = jnp.broadcast_to(hm, (256, 128))
        ones[1024 + 32 * h:1056 + 32 * h] = jnp.broadcast_to(hm, (32, 128))


def head_lanes():
    spot = lanes((1, 128))
    return spot, [(spot // 32 == h).astype(BF16) for h in range(4)], [(spot // 3 == h).astype(BF16) for h in range(4)]


def project(ws, tokens, land_row, blocked_row, gain, wqkv, operands):
    qst, qpl, kpl, vst, lqx, lk, mk, mkt = operands
    nq = qpl.shape[1]
    spot, hms, threes = head_lanes()
    xn = jnp.concatenate([norm(tokens[w], gain) for w in ws], axis=0)
    xq = xn if nq == W else jnp.concatenate([xn[0:nq], xn[W:W + nq]], axis=0)
    for c in range(6):
        cols = slice(c * 256, (c + 1) * 256)
        if c < 2:
            r = (dot(xq, wqkv[:, cols]) * SCALE).astype(BF16)
            for a in range(2):
                ra = r[a * nq:(a + 1) * nq]
                qpl[a, :, cols] = ra
                for gl in range(2):
                    for h in range(4):
                        qst[a, 2 * c + gl, h * nq:(h + 1) * nq] = ra[:, gl * 128:(gl + 1) * 128] * hms[h]
        else:
            r = dot(xn, wqkv[:, cols]).astype(BF16)
            for a in range(2):
                ra = r[a * W:(a + 1) * W]
                if c < 4:
                    kpl[a, :, (c - 2) * 256:(c - 1) * 256] = ra
                    continue
                for gl in range(2):
                    g = 2 * (c - 4) + gl
                    for h in range(4):
                        vm = ra[:, gl * 128:(gl + 1) * 128] * hms[h]
                        vst[a, g, 256 * h:256 * h + 256] = vm[0:256]
                        vst[a, g, 1024 + 32 * h:1056 + 32 * h] = vm[256:288]
    eye = rows((W, W)) == lanes((W, W))
    for a, w in enumerate(ws):
        land = jnp.broadcast_to(jnp.sum(jnp.where(eye, land_row(w), 0.0), axis=1, keepdims=True), (W, 128))
        lk[a] = land
        lq = land[0:nq].astype(BF16)
        for h in range(4):
            lqx[a, h * nq:(h + 1) * nq] = lq * threes[h]
        mm = jnp.where(eye[0:nq], 0.0, blocked_row(w))
        mk[a] = mm[:, 0:256]
        mkt[a] = jnp.concatenate([mm[:, 256:288]] * 4, axis=1)


def attend(ws, own, out_row, ho, common, operands):
    brow, ones, s0, s1, t0, t1, p0, p1 = common
    qst, qpl, kpl, vst, lqx, lk, mk, mkt = operands
    nq = qpl.shape[1]
    spot, hms, threes = head_lanes()
    ss, ts, ps = (s0, s1), (t0, t1), (p0, p1)

    def q_step(n):
        a, g, b = n // 4, n % 4, n % 2
        k = kpl[a, :, g * 128:(g + 1) * 128]
        kx = (lk[a] * brow[g:g + 1]).astype(BF16)
        ss[b][...] = dot_t(jnp.concatenate([qst[a, g], lqx[a]], axis=1), jnp.concatenate([k[0:256], kx[0:256]], axis=1))
        kt = jnp.concatenate([
            jnp.concatenate([k[256:288] * hms[h] for h in range(4)], axis=0),
            jnp.concatenate([kx[256:288] * threes[h] for h in range(4)], axis=0)], axis=1)
        lq = lk[a, 0:nq].astype(BF16)
        ts[b][...] = dot_t(jnp.concatenate([qpl[a, :, g * 128:(g + 1) * 128], lq], axis=1), kt)

    def s_step(n):
        a, b = n // 4, n % 2
        for r in range(0, own, 16):
            at = slice(r, min(r + 16, own))
            size = at.stop - r
            t = ts[b][at] + mkt[a, at]
            mask = mk[a, at]
            tops = []
            for h in range(4):
                s = ss[b][h * nq + r:h * nq + r + size] + mask
                m = jnp.maximum(jnp.maximum(s[:, :128], s[:, 128:]), jnp.where(spot // 32 == h, t, -3e38))
                m = jnp.max(m, axis=-1, keepdims=True)
                ps[b][at, h * 256:(h + 1) * 256] = jnp.exp2(s - m).astype(BF16)
                tops.append(m)
            top = jnp.where(spot < 32, tops[0], jnp.where(spot < 64, tops[1], jnp.where(spot < 96, tops[2], tops[3])))
            ps[b][at, 1024:1152] = jnp.exp2(t - top).astype(BF16)

    def v_step(n):
        a, g, b = n // 4, n % 4, n % 2
        o = dot(ps[b][0:own], jnp.concatenate([vst[a, g], ones[...]], axis=1))
        ho[pl.ds(out_row(ws[a]), own), g * 128:(g + 1) * 128] = (o[:, :128] / o[:, 128:]).astype(BF16)

    for n in range(10):
        if n < 8:
            q_step(n)
        if 1 <= n < 9:
            s_step(n - 1)
        if n >= 2:
            v_step(n - 2)


def feed_forward(res, gain, wup, wdown):
    xn = norm(res, gain)
    acc = res
    for c in range(4):
        hidden = gelu(dot(xn, wup[:, c * 512:(c + 1) * 512])).astype(BF16)
        acc = acc + dot(hidden, wdown[c * 512:(c + 1) * 512, :])
    return acc.astype(BF16)


def fetch(pairs, sems):
    copies = [pltpu.make_async_copy(src, dst, sems.at[n]) for n, (src, dst) in enumerate(pairs)]
    for c in copies:
        c.start()
    return copies


def pack_lon_body(first, last, land, pad, to_right, to_left):
    for strip, c0, to in ((last, 30, to_right), (first, 0, to_left)):
        to[0:HALO] = strip[...].reshape(HALO, 512)
        zero = jnp.zeros((10, 128), F32)
        a = jnp.concatenate([land[c0:c0 + 6].astype(F32), jnp.zeros((6, 80), F32)], axis=1)
        b = jnp.concatenate([pad[c0:c0 + 6].astype(F32), jnp.zeros((6, 80), F32)], axis=1)
        a = jnp.concatenate([a, zero], axis=0)
        b = jnp.concatenate([b, zero], axis=0)
        to[HALO:PAY] = jnp.concatenate([a, b, jnp.zeros((16, 256), F32)], axis=1).astype(BF16)


def wide_masks(land, pad, left, right, wide):
    l, r = left[HALO:PAY].astype(F32), right[HALO:PAY].astype(F32)
    for n, own in enumerate((land, pad)):
        wide[n, 0:6, 0:48] = l[0:6, 128 * n:128 * n + 48]
        wide[n, 6:42, 0:48] = own[...].astype(F32)
        wide[n, 42:48, 0:48] = r[0:6, 128 * n:128 * n + 48]


def pack_lat_body(x_low, x_high, left, right, land, pad, to_down, to_up, buf, wide):
    wide_masks(land, pad, left, right, wide)
    for to, xs, r0 in ((to_down, x_high, 42), (to_up, x_low, 0)):
        x0 = 10 if r0 else 0
        for l in range(2):
            for e in range(48):
                row = 6 * (48 * l + e)
                if e < 6 or e >= 42:
                    src, c = (left, e) if e < 6 else (right, e - 42)
                    a = (6 * l + c) * 48 + (32 if r0 else 0)
                    buf[row:row + 6] = src[a:a + 16].astype(F32)[x0:x0 + 6]
                else:
                    buf[row:row + 6] = xs[l, e - 6].astype(F32)[x0:x0 + 6]
        to[0:HALO] = buf[...].astype(BF16)
        pick = (lanes((16, 48)) == rows((16, 48)) + r0).astype(BF16)
        a = dot_t(pick, wide[0].astype(BF16)[:, 0:48])
        b = dot_t(pick, wide[1].astype(BF16)[:, 0:48])
        zero = jnp.zeros((16, 80), F32)
        tail = jnp.concatenate([a, zero, b, zero, jnp.zeros((16, 256), F32)], axis=1)
        to[HALO:PAY] = jnp.where(rows((16, 512)) < 6, tail, 0.0).astype(BF16)


def inner_attention_body(x_hbm, land, pad, g1, wqkv_hbm, bias, ho, xg, x, wqkv, sems, *scratch):
    parts = [(l, jc) for jc in range(2) for l in range(2)]
    copies = fetch([(x_hbm.at[l, pl.ds(6 + 12 * jc, 12)], x.at[n]) for n, (l, jc) in enumerate(parts)] + [(wqkv_hbm, wqkv)], sems)
    common, operands = scratch[:8], scratch[8:]
    attend_setup(bias, common[0], common[1])
    for n, (l, jc) in enumerate(parts):
        copies[n].wait()
        for c in range(12):
            v = x[n, c].astype(F32)
            for i in range(3):
                xg[jc * 3 + i, l * 144 + 12 * c:l * 144 + 12 * c + 12, :] = v[6 + 12 * i:18 + 12 * i]
    copies[4].wait()

    gain = g1[...]
    land_b, pad_b = halves(land), halves(pad)

    def row_of(cells, w):
        lane = lanes((1, W)) % 144
        here = rows((36, W)) == 6 + (w // 3) * 12 + lane // 12
        pick = (rows((48, W)) == 6 + (w % 3) * 12 + lane % 12).astype(BF16)
        return jnp.sum(jnp.where(here, dot(cells, pick), 0.0), axis=0, keepdims=True)

    @pl.loop(0, 3)
    def _(n):
        ws = (2 * n, 2 * n + 1)
        project(ws, xg, lambda w: row_of(land_b, w), lambda w: row_of(pad_b, w) * NEG, gain, wqkv, operands)
        attend(ws, W, lambda w: pl.multiple_of(w * W, 32), ho, common, operands)


def inner_rest_body(ho, x, wout, g2, wup_hbm, wdown_hbm, out, edge, att, nat, wup, wdown, sems):
    copies = fetch(((wup_hbm, wup), (wdown_hbm, wdown)), sems)

    @pl.loop(0, 2)
    def _(n):
        h = ho[pl.ds(pl.multiple_of(n * 3 * W, 32), 3 * W), :]
        for c in range(2):
            r = dot(h, wout[:, c * 256:(c + 1) * 256])
            for i in range(3):
                att[n * 3 + i, :, c * 256:(c + 1) * 256] = r[i * W:(i + 1) * W]

    @pl.loop(0, 4)
    def _(n):
        l, jc = n // 2, n % 2
        for c in range(12):
            k = n * 12 + c
            for i in range(3):
                nat[k, 6 + 12 * i:18 + 12 * i] = att.at[jc * 3 + i, pl.ds(pl.multiple_of(l * 144, 8), 144), :][12 * c:12 * c + 12]
            nat[k] = nat[k] + x[l, 6 + jc * 12 + c].astype(F32)
            edge[k, 0] = nat[k, 0:8]
            edge[k, 1] = nat[k, 40:48]

    for c in copies:
        c.wait()
    gain = g2[...]

    @pl.loop(0, 2)
    def _(n):
        res = nat[pl.ds(n * 24, 24), 8:40, :].reshape(768, 512)
        out[pl.ds(n * 24, 24)] = feed_forward(res, gain, wup, wdown).reshape(24, 32, 512)


def edge_windows():
    tens = [(i, j) for i in (1, 2, 3) for j in (0, 3)] + [(i, j) for i in (0, 4) for j in (1, 2)]
    return tens + [(i, j) for i in (0, 4) for j in (0, 3)]


def pieces(i, j):
    runs = {0: ((6, 6), (0, 6)), 4: ((48, 6), (54, 6))}.get(i, ((12 * i, 12),))
    cols = {0: (range(6, 12), range(0, 6)), 3: (range(36, 42), range(42, 48))}.get(j, (range(12 * j, 12 * j + 12),))
    return [(l, e, f, n) for es in cols for f, n in runs for l in range(2) for e in es]


def cell_maps():
    e_of, f_of = [], []
    for i, j in edge_windows():
        e_of.append([e for l, e, f, n in pieces(i, j) for _ in range(n)])
        f_of.append([f + a for l, e, f, n in pieces(i, j) for a in range(n)])
    return np.array(e_of, np.int32)[:, None], np.array(f_of, np.int32)[:, None]


def border_body(e_map, f_map, land, pad, x_hbm, left_hbm, right_hbm, up_hbm, down_hbm, inner_hbm, edge_hbm, g1, wqkv_hbm, bias, wout_hbm, g2, wup_hbm,
                wdown_hbm, out_hbm, x, left, right, up, down, edge, wqkv, out, xg, ho, att, nat_s, nat_i, wide, inner, wout, wup, wdown, sems, *scratch):
    sides = (slice(0, 6), slice(30, 36))
    copies = fetch([(x_hbm.at[:, pl.ds(0, 6)], x.at[:, pl.ds(0, 6)]), (x_hbm.at[:, pl.ds(30, 6)], x.at[:, pl.ds(30, 6)]),
                    (left_hbm, left), (right_hbm, right), (wqkv_hbm, wqkv), (up_hbm, up), (down_hbm, down),
                    (x_hbm.at[:, pl.ds(6, 24)], x.at[:, pl.ds(6, 24)]), (wout_hbm, wout), (edge_hbm, edge), (inner_hbm, inner),
                    (wup_hbm, wup), (wdown_hbm, wdown)], sems)
    common, operands = scratch[:8], (scratch[8:16], scratch[16:24])
    attend_setup(bias, common[0], common[1])
    lat = lax.axis_index("lat")
    first_row, last_row = lat == 0, lat == lax.axis_size("lat") - 1
    for c in copies[:4]:
        c.wait()
    wide_masks(land, pad, left, right, wide)
    wins = edge_windows()
    gain1 = g1[...]

    def gather(w):
        i, j = wins[w]
        row = 0
        for l, e, f, n in pieces(i, j):
            if f < 6 or f >= 54:
                a = 6 * (48 * l + e)
                lo = a // 16 * 16
                seg = (up if f < 6 else down)[lo:lo + 32].astype(F32)[a - lo:a - lo + 6]
            elif 6 <= e < 42:
                seg = x[l, e - 6].astype(F32)[f - 6:f - 6 + n]
            else:
                src, c = (left, e) if e < 6 else (right, e - 42)
                a = (6 * l + c) * 48
                seg = src[a:a + 48].astype(F32)[f - 6:f - 6 + n]
            xg[w, row:row + n, :] = seg
            row += n

    masks = [wide[n].astype(BF16)[:, 0:48] for n in range(2)]

    def row_of(n, w):
        e, f = e_map[w], f_map[w]
        pick_f = (rows((48, W)) == f - 6).astype(BF16)
        pick_e = (rows((48, W)) == e).astype(BF16)
        far = jnp.where(f < 6, f, f - 54 + 16)
        far = jnp.where((f < 6) | (f >= 54), far, 99)
        mid = jnp.sum(jnp.where(rows((48, W)) == e, dot(masks[n], pick_f), 0.0), axis=0, keepdims=True)
        beyond = jnp.concatenate([up[HALO:PAY, 128 * n:128 * n + 48], down[HALO:PAY, 128 * n:128 * n + 48]], axis=0)
        return mid + jnp.sum(jnp.where(rows((32, W)) == far, dot(beyond, pick_e), 0.0), axis=0, keepdims=True)

    def blocked(w):
        f = f_map[w]
        over = ((f < 6) & first_row) | ((f >= 54) & last_row)
        return jnp.where(over | (row_of(1, w) > 0.5), NEG, 0.0)

    for w in range(6):
        gather(w)
    for c in copies[4:8]:
        c.wait()
    for w in range(6, 14):
        gather(w)

    def start(n, to):
        project((2 * n, 2 * n + 1), xg, lambda w: row_of(0, w), blocked, gain1, wqkv, operands[to])

    def finish(n, own, at):
        attend((2 * n, 2 * n + 1), own, lambda w: pl.multiple_of(w * 144, 16), ho, common, operands[at])

    start(0, 0)

    @pl.loop(0, 2)
    def _(m):
        start(2 * m + 1, 1)
        finish(2 * m, 144, 0)
        start(2 * m + 2, 0)
        finish(2 * m + 1, 144, 1)

    start(5, 1)
    finish(4, 144, 0)
    start(6, 0)
    finish(5, 72, 1)
    finish(6, 72, 0)

    for c in copies[8:]:
        c.wait()

    @pl.loop(0, 2)
    def _(n):
        h = ho[pl.ds(pl.multiple_of(n * 1008, 16), 1008), :]
        for c in range(2):
            a = dot(h, wout[:, c * 256:(c + 1) * 256])
            for i in range(7):
                att[7 * n + i, :, c * 256:(c + 1) * 256] = a[144 * i:144 * i + 144]

    side = {c: s for s, c in enumerate(list(range(6)) + list(range(30, 36)))}
    for w, (i, j) in enumerate(wins):
        row = 0
        for l, e, f, n in pieces(i, j):
            if row == (144 if w < 10 else 72):
                break
            c, r = e - 6, f - 6
            seg = att[w, row:row + n, :]
            if c in side:
                nat_s[l * 12 + side[c], r:r + n, :] = seg
            elif r == 0:
                nat_i[l * 24 + c - 6, 0, 0:6, :] = seg
            else:
                nat_i[l * 24 + c - 6, 1, 2:8, :] = seg
            row += n
    gain2 = g2[...]

    @pl.loop(0, 2)
    def _(l):
        xs = jnp.concatenate([x[l, 0:6], x[l, 30:36]], axis=0).astype(F32)
        res = nat_s[pl.ds(12 * l, 12)] + xs
        y = feed_forward(res.reshape(576, 512), gain2, wup, wdown).reshape(12, 48, 512)
        out[l, 0:6] = y[0:6]
        out[l, 30:36] = y[6:12]

    sent = [pltpu.make_async_copy(out.at[:, pl.ds(at.start, 6)], out_hbm.at[:, pl.ds(at.start, 6)], sems.at[n]) for n, at in enumerate(sides)]
    for c in sent:
        c.start()

    @pl.loop(0, 2)
    def _(l):
        xs = x[l, 6:30].astype(F32)
        at = nat_i[pl.ds(24 * l, 24)]
        ed = edge[pl.ds(24 * l, 24)]
        low = jnp.where(rows((1, 8, 512)) < 6, at[:, 0] + xs[:, 0:8], ed[:, 0])
        high = jnp.where(rows((1, 8, 512)) >= 2, at[:, 1] + xs[:, 40:48], ed[:, 1])
        res = jnp.concatenate([low.reshape(192, 512), high.reshape(192, 512)], axis=0)
        y = feed_forward(res, gain2, wup, wdown).astype(F32)
        full = jnp.concatenate([y[0:192].reshape(24, 8, 512), inner[pl.ds(24 * l, 24)].astype(F32), y[192:384].reshape(24, 8, 512)], axis=1)
        out[l, 6:30] = full.astype(BF16)

    sent.append(pltpu.make_async_copy(out.at[:, pl.ds(6, 24)], out_hbm.at[:, pl.ds(6, 24)], sems.at[2]))
    sent[2].start()
    for c in sent:
        c.wait()


VM = pl.BlockSpec(memory_space=pltpu.VMEM)
SM = pl.BlockSpec(memory_space=pltpu.SMEM)
HBM = pl.BlockSpec(memory_space=pl.ANY)


def params():
    return pltpu.CompilerParams(vmem_limit_bytes=LIMIT)


def cost(flops, nbytes):
    return pl.CostEstimate(flops=flops, bytes_accessed=nbytes, transcendentals=0)


def pack_lon(xt, land, pad):
    strip = jax.ShapeDtypeStruct((PAY, 512), BF16)
    return pl.pallas_call(
        pack_lon_body, grid=(1,), out_shape=[strip] * 2,
        in_specs=[pl.BlockSpec((2, 6, 48, 512), lambda i: (0, 0, 0, 0)), pl.BlockSpec((2, 6, 48, 512), lambda i: (0, 5, 0, 0)), VM, VM],
        out_specs=[VM] * 2, compiler_params=pltpu.CompilerParams(vmem_limit_bytes=LIMIT), cost_estimate=cost(1, 2 * MB))(xt, xt, land, pad)


def pack_lat(xt, left, right, land, pad):
    strip = jax.ShapeDtypeStruct((PAY, 512), BF16)
    return pl.pallas_call(
        pack_lat_body, grid=(1,), out_shape=[strip] * 2,
        in_specs=[pl.BlockSpec((2, 36, 16, 512), lambda i: (0, 0, 0, 0)), pl.BlockSpec((2, 36, 16, 512), lambda i: (0, 0, 2, 0)), VM, VM, VM, VM],
        out_specs=[VM] * 2, scratch_shapes=[pltpu.VMEM((HALO, 512), F32), pltpu.VMEM((2, 48, 128), F32)],
        compiler_params=pltpu.CompilerParams(vmem_limit_bytes=LIMIT), cost_estimate=cost(1, 4 * MB))(xt, xt, left, right, land, pad)


def inner_attention(xt, land, pad, g1, wqkv, bias):
    return pl.pallas_call(
        inner_attention_body, out_shape=jax.ShapeDtypeStruct((6 * W, 512), BF16),
        in_specs=[HBM, VM, VM, VM, HBM, SM], out_specs=VM,
        scratch_shapes=[pltpu.VMEM((6, W, 512), F32), pltpu.VMEM((4, 12, 48, 512), BF16), pltpu.VMEM((512, 1536), BF16),
                        pltpu.SemaphoreType.DMA((5,))] + attend_scratch(W) + operand_scratch(W),
        compiler_params=params(), cost_estimate=cost(22 * 10**9, 8 * MB))(xt, land, pad, g1, wqkv, bias)


def inner_rest(ho, xt, wout, g2, wup, wdown):
    return pl.pallas_call(
        inner_rest_body, out_shape=[jax.ShapeDtypeStruct((48, 32, 512), BF16), jax.ShapeDtypeStruct((48, 2, 8, 512), F32)],
        in_specs=[VM] * 4 + [HBM] * 2, out_specs=[VM] * 2,
        scratch_shapes=[pltpu.VMEM((6, W, 512), F32), pltpu.VMEM((48, 48, 512), F32), pltpu.VMEM((512, 2048), BF16), pltpu.VMEM((2048, 512), BF16),
                        pltpu.SemaphoreType.DMA((2,))],
        compiler_params=params(), cost_estimate=cost(16 * 10**9, 10 * MB))(ho, xt, wout, g2, wup, wdown)


def border(land, pad, xt, left, right, up, down, inner, edge, g1, wqkv, bias, wout, g2, wup, wdown):
    e_map, f_map = cell_maps()
    return pl.pallas_call(
        border_body, out_shape=jax.ShapeDtypeStruct((2, 36, 48, 512), BF16),
        in_specs=[VM] * 4 + [HBM] * 7 + [VM, HBM, SM, HBM, VM, HBM, HBM], out_specs=HBM,
        scratch_shapes=[
            pltpu.VMEM((2, 36, 48, 512), BF16),
            *[pltpu.VMEM((PAY, 512), BF16)] * 4,
            pltpu.VMEM((48, 2, 8, 512), F32),
            pltpu.VMEM((512, 1536), BF16),
            pltpu.VMEM((2, 36, 48, 512), BF16),
            pltpu.VMEM((14, W, 512), F32),
            pltpu.VMEM((14 * 144, 512), BF16),
            pltpu.VMEM((14, 144, 512), F32),
            pltpu.VMEM((24, 48, 512), F32),
            pltpu.VMEM((48, 2, 8, 512), F32),
            pltpu.VMEM((2, 48, 128), F32),
            pltpu.VMEM((48, 32, 512), BF16),
            pltpu.VMEM((512, 512), BF16),
            pltpu.VMEM((512, 2048), BF16),
            pltpu.VMEM((2048, 512), BF16),
            pltpu.SemaphoreType.DMA((13,)),
        ] + attend_scratch(144) + operand_scratch(144) * 2,
        compiler_params=params(), cost_estimate=cost(40 * 10**9, 20 * MB))(
            jnp.asarray(e_map), jnp.asarray(f_map), land, pad, xt, left, right, up, down, inner, edge, g1, wqkv, bias, wout, g2, wup, wdown)


def from_behind(value, axis, by):
    devices = lax.axis_size(axis)
    return lax.ppermute(value, axis, [(i, (i + by) % devices) for i in range(devices)])


def on_device(latent_field, land_mask, padded, norm1_gain, qkv_weight, land_bias, out_weight, norm2_gain, up_weight, down_weight):
    xt = latent_field.transpose(0, 2, 1, 3)
    land, pad = land_mask.T, padded.T
    g1, g2 = norm1_gain.reshape(1, 512), norm2_gain.reshape(1, 512)
    to_right, to_left = pack_lon(xt, land, pad)
    left, right = from_behind(to_right, "lon", 1), from_behind(to_left, "lon", -1)
    ho = inner_attention(xt, land, pad, g1, qkv_weight, land_bias)
    ho, left, right = lax.optimization_barrier((ho, left, right))
    to_down, to_up = pack_lat(xt, left, right, land, pad)
    up, down = from_behind(to_down, "lat", 1), from_behind(to_up, "lat", -1)
    inner, edge = inner_rest(ho, xt, out_weight, g2, up_weight, down_weight)
    y = border(land, pad, xt, left, right, up, down, inner, edge, g1, qkv_weight, land_bias, out_weight, g2, up_weight, down_weight)
    return y.transpose(0, 2, 1, 3)


def solution(mesh):
    spec = P(None, "lat", "lon", None)
    placed = (spec, P("lat", "lon"), P("lat", "lon")) + (P(),) * 7
    return jax.shard_map(on_device, mesh=mesh, in_specs=placed, out_specs=spec, check_vma=False)
```
